32 devices in a mesh: hi: 4 (over y, core), lo: 8 (over z, x).
Axes of the slice: x: 2, y: 2, z: 4, core: 2. Of those that a mesh axis runs over, the one named last changes fastest.
Arguments:
- panel: float32 [262144, 128], P(('hi', 'lo')), may hold values from -6 to 6
- row_signs: float32 [262144, 1], P(('hi', 'lo')), may hold values from -4 to 4
- sample_rows: int32 [1024], replicated, may hold values from 0 to 262143, as said below
Outputs:
- sketch: float32 [1024, 128], P(('hi', 'lo'))
The draws below stay inside these ranges and needn't reach their ends.
Inputs may be any that keep to these rules, and one draw needn't show every extreme that they name: `sample_rows`: repeats may occur; they fall very unevenly on the devices that hold the rows.
All inputs are finite; a program needn't handle non-finite values.
Results may differ from the reference program's by a relative error of at most 0.000098.
Values sent between devices are 32-bit elements; how exact they have to be, the bound alone decides.
A program may use at most 64 MiB of HBM per device.

```python
import jax
import jax.numpy as jnp

ROWS_DEV = 8192
COLS = 128
ROWS = 262144
SAMPLE = 1024
N_HI = 4
N_LO = 8


def draw_sample_rows(key, part):
    first_key, second_key = jax.random.split(jax.random.fold_in(key, 11))
    ndev = N_HI * N_LO
    picks = jax.random.randint(first_key, (SAMPLE,), 0, ndev)
    owner = (picks * picks + picks) // ndev
    within = jax.random.randint(second_key, (SAMPLE,), 0, ROWS_DEV)
    rows = (owner * ROWS_DEV + within).astype(jnp.int32)
    rows = rows.at[0].set(jnp.int32(0))
    rows = rows.at[SAMPLE - 1].set(jnp.int32(ROWS - 1))
    return rows


def levels(rng, extent, shards, least, high):
    gain = 1.0
    for dim, shards_of in shards:
        draws = jax.random.uniform(jax.random.fold_in(jax.random.fold_in(rng, 6), dim), (shards_of,), jnp.float32, least / len(shards), high / len(shards))
        gain = gain * jnp.repeat(jnp.exp(draws), extent[dim] // shards_of).reshape((-1,) + (1,) * (len(extent) - 1 - dim))
    return gain


def bell_draw(key, dims, spread, reach, cuts=(), held_as=jnp.bfloat16):
    drawn = spread * jax.random.normal(key, dims, jnp.float32)
    if cuts:
        drawn = drawn * levels(key, dims, cuts, -0.22, 0.18)
    return jnp.clip(drawn, -reach, reach).astype(held_as)


def setup_inputs(seed: int = 0) -> dict:
    seeds = jax.random.split(jax.random.key(seed), 4)
    panel = bell_draw(seeds[0], (ROWS, COLS), 1.0, 6.0, ((0, 32),), jnp.float32)
    row_signs = bell_draw(seeds[1], (ROWS, 1), 1.0, 4.0, ((0, 32),), jnp.float32)
    sample_rows = draw_sample_rows(jax.random.fold_in(seeds[3], 71), 0)
    return {"panel": panel, "row_signs": row_signs, "sample_rows": sample_rows}


def reference(panel, row_signs, sample_rows):
    total = panel.shape[0]
    width = panel.shape[1]
    field = row_signs * panel
    half = 1
    while half < total:
        shaped = field.reshape(total // (2 * half), 2, half, width)
        first = shaped[:, 0]
        second = shaped[:, 1]
        field = jnp.stack([first + second, first - second], axis=1).reshape(total, width)
        half = half * 2
    picked = jnp.take(field, sample_rows, axis=0)
    return picked / jnp.sqrt(jnp.float32(total))
```

```python
import functools
import math

import jax
import jax.numpy as jnp
from jax import lax
from jax.experimental import pallas as pl
from jax.experimental.pallas import tpu as pltpu
from jax.sharding import PartitionSpec as P

MESH = pl.DeviceIdType.MESH
LOW = 256
LANES = 128
TILE = 8


def parity_sign(bits):
    shift = 16
    while shift:
        bits = bits ^ (bits >> shift)
        shift //= 2
    return (1 - 2 * (bits & 1)).astype(jnp.float32)


def kernel(hi_count, lo_count, panel_hbm, signs_hbm, rows_hbm, picks_hbm, out_ref,
           panel, signs_ref, rows_ref, picks_ref, field, had, sgn, terms, mine, got_a, got_b, got_c, last,
           load_sem, small_sem, send_a, recv_a, send_b, recv_b, send_c, recv_c):
    count = panel.shape[0]
    blocks = count // LOW
    share = out_ref.shape[0]
    total = count * hi_count * lo_count
    side = 2 ** ((lo_count.bit_length() - 1) // 2)
    depth = lo_count // side
    plane = (hi_count // 2) * side
    hi, lo = lax.axis_index("hi"), lax.axis_index("lo")
    me = hi * lo_count + lo
    core = hi % 2
    spot = (hi // 2) * side + lo % side
    level = lo // side

    def place(core_to, level_to, spot_to):
        return ((spot_to // side) * 2 + core_to, level_to * side + spot_to % side)

    partner = place(1 - core, level, spot)
    peers_plane = [place(core, level, spot ^ j) for j in range(plane)]
    peers_depth = [place(core, level ^ r, spot) for r in range(depth)]

    loads = load_sem.shape[0]
    rows_load = count // loads
    small = [pltpu.make_async_copy(signs_hbm, signs_ref, small_sem.at[0]),
             pltpu.make_async_copy(picks_hbm, picks_ref, small_sem.at[1]),
             pltpu.make_async_copy(rows_hbm, rows_ref, small_sem.at[2])]
    for copy in small:
        copy.start()

    def load(i):
        part = pl.ds(i * rows_load, rows_load)
        return pltpu.make_async_copy(panel_hbm.at[part], panel.at[part], load_sem.at[i])

    for i in range(loads):
        load(i).start()

    barrier = pltpu.get_barrier_semaphore()
    greet = [partner] + peers_plane[1:] + peers_depth[1:]
    for device in greet:
        pl.semaphore_signal(barrier, inc=1, device_id=device, device_id_type=MESH)

    left = lax.broadcasted_iota(jnp.int32, (LOW, LOW), 0)
    right = lax.broadcasted_iota(jnp.int32, (LOW, LOW), 1)
    had[...] = parity_sign(left & right).astype(jnp.bfloat16)

    for copy in small:
        copy.wait()

    weight = parity_sign((picks_ref[...] // count) & me) * (1.0 / math.sqrt(total))
    for g in range(weight.shape[0]):
        sgn[pl.ds(g * LANES, LANES), :] = jnp.broadcast_to(weight[g:g + 1, :], (LANES, LANES)).T

    @pl.loop(0, loads)
    def _(i):
        load(i).wait()
        for step in range(blocks // loads):
            a = i * (blocks // loads) + step
            parts = []
            for h in range(LOW // LANES):
                line = signs_ref[pl.ds(a * (LOW // LANES) + h, 1), :]
                wide = jnp.broadcast_to(line, (LANES, LANES)).T
                parts.append(panel[pl.ds(a * LOW + h * LANES, LANES), :] * wide)
            block = jnp.concatenate(parts, axis=0)
            big = block.astype(jnp.bfloat16)
            small = (block - big.astype(jnp.float32)).astype(jnp.bfloat16)
            both = jnp.concatenate([big, small], axis=1)
            done = jnp.dot(had[...], both, preferred_element_type=jnp.float32)
            field[pl.ds(a * LOW, LOW), :] = done[:, :LANES] + done[:, LANES:]

    @pl.loop(0, LOW // TILE)
    def _(p):
        parts = [field[pl.ds(b * LOW + p * TILE, TILE), :] for b in range(blocks)]
        half = 1
        while half < blocks:
            for b in range(blocks):
                if not b & half:
                    x, y = parts[b], parts[b + half]
                    parts[b], parts[b + half] = x + y, x - y
            half *= 2
        for b in range(blocks):
            field[pl.ds(b * LOW + p * TILE, TILE), :] = parts[b]

    pl.semaphore_wait(barrier, len(greet))

    def gather(dst, core_to, level_to):
        @pl.loop(0, plane)
        def _(j):
            hi_to, lo_to = place(core_to, level_to, spot ^ j)
            start = (hi_to * lo_count + lo_to) * share
            for s in range(share):
                row = rows_ref[start + s] & (count - 1)
                dst[pl.ds(j * share + s, 1), :] = field[pl.ds(row, 1), :]
            part = pl.ds(j * share, share)
            dst[part, :] = dst[part, :] * sgn[pl.ds(start, share), :]

    def remote(src, dst, send, recv, device):
        return pltpu.make_async_remote_copy(
            src_ref=src, dst_ref=dst, send_sem=send, recv_sem=recv,
            device_id=device, device_id_type=MESH)

    levels = range(depth)
    sent_a, sent_b = {}, {}

    def send_pair(c):
        gather(terms.at[c], 1 - core, c)
        sent_a[c] = remote(terms.at[c], got_a.at[c], send_a.at[c], recv_a.at[c], partner)
        sent_a[c].start()
        if c:
            send_plane(c - 1)
        gather(mine.at[c], core, c)

    def send_plane(c):
        sent_a[c].wait_recv()
        for j in list(range(1, plane)) + [0]:
            part = pl.ds(j * share, share)
            mine[c, part, :] = mine[c, part, :] + got_a[c, part, :]
            if j:
                sent_b[c, j] = remote(mine.at[c, part], got_b.at[c, part],
                                      send_b.at[c, j], recv_b.at[c, j], peers_plane[j])
                sent_b[c, j].start()

    def to_level(c):
        return remote(last.at[c], got_c.at[level], send_c.at[c], recv_c.at[level],
                      place(core, c, spot))

    def send_level(c):
        rows = mine[c, pl.ds(0, share), :]
        for j in range(1, plane):
            sent_b[c, j].wait_recv()
            rows = rows + got_b[c, pl.ds(j * share, share), :]
        last[c] = rows

        @pl.when(level != c)
        def _():
            to_level(c).start()

    for c in levels:
        send_pair(c)
    send_plane(depth - 1)
    for c in levels:
        send_level(c)
    result = last[level]
    for r in range(1, depth):
        other = level ^ r
        remote(last.at[other], got_c.at[other], send_c.at[other], recv_c.at[other],
               place(core, other, spot)).wait_recv()
        result = result + got_c[other]
    out_ref[...] = result
    for c in levels:
        sent_a[c].wait_send()
        for j in range(1, plane):
            sent_b[c, j].wait_send()

        @pl.when(level != c)
        def _():
            to_level(c).wait_send()


def body(panel, row_signs, sample_rows):
    count, width = panel.shape
    hi_count, lo_count = lax.axis_size("hi"), lax.axis_size("lo")
    kept = sample_rows.shape[0]
    share = kept // (hi_count * lo_count)
    side = 2 ** ((lo_count.bit_length() - 1) // 2)
    depth = lo_count // side
    plane = (hi_count // 2) * side
    loads = 2
    vmem = pl.BlockSpec(memory_space=pltpu.VMEM)
    dma = pltpu.SemaphoreType.DMA
    f32 = jnp.float32
    chunk = (depth, plane * share, width)
    return pl.pallas_call(
        functools.partial(kernel, hi_count, lo_count),
        out_shape=pltpu.VMEM((share, width), f32),
        in_specs=[pl.BlockSpec(memory_space=pltpu.HBM)] * 4,
        out_specs=vmem,
        scratch_shapes=[
            pltpu.VMEM((count, width), f32),
            pltpu.VMEM((count // LANES, LANES), f32),
            pltpu.SMEM((kept,), jnp.int32),
            pltpu.VMEM((kept // LANES, LANES), jnp.int32),
            pltpu.VMEM((count, width), f32),
            pltpu.VMEM((LOW, LOW), jnp.bfloat16),
            pltpu.VMEM((kept, width), f32),
            pltpu.VMEM(chunk, f32),
            pltpu.VMEM(chunk, f32),
            pltpu.VMEM(chunk, f32),
            pltpu.VMEM(chunk, f32),
            pltpu.VMEM((depth, share, width), f32),
            pltpu.VMEM((depth, share, width), f32),
            dma((loads,)), dma((3,)),
            dma((depth,)), dma((depth,)),
            dma((depth, plane)), dma((depth, plane)),
            dma((depth,)), dma((depth,)),
        ],
        compiler_params=pltpu.CompilerParams(
            collective_id=0, has_side_effects=True, vmem_limit_bytes=60 * 2**20),
        cost_estimate=pl.CostEstimate(
            flops=2 * count * LOW * 2 * width, bytes_accessed=count * width * 4, transcendentals=0),
    )(panel, row_signs.reshape(count // LANES, LANES), sample_rows,
      sample_rows.reshape(kept // LANES, LANES))


def solution(mesh):
    placed = (P(("hi", "lo"), None), P(("hi", "lo"), None), P())
    return jax.shard_map(
        body, mesh=mesh, in_specs=placed, out_specs=P(("hi", "lo"), None), check_vma=False
    )
```

```python
import functools
import math

import jax
import jax.numpy as jnp
from jax import lax
from jax.experimental import pallas as pl
from jax.experimental.pallas import tpu as pltpu
from jax.sharding import PartitionSpec as P

MESH = pl.DeviceIdType.MESH
LOW = 256
LANES = 128
TILE = 8
FUSED = 8
CUTS = (0, 2, 5, 8)


def parity_sign(bits):
    shift = 16
    while shift:
        bits = bits ^ (bits >> shift)
        shift //= 2
    return (1 - 2 * (bits & 1)).astype(jnp.float32)


def kernel(hi_count, lo_count, panel_hbm, signs_hbm, rows_hbm, picks_hbm, out_ref,
           panel, signs_ref, rows_ref, picks_ref, field, had, wide, weights_ref, sgn, terms, mine, got_a, got_b, got_c, last,
           load_sem, small_sem, send_a, recv_a, send_b, recv_b, send_c, recv_c):
    count = panel.shape[0]
    share = out_ref.shape[0]
    kept = rows_ref.shape[0]
    total = count * hi_count * lo_count
    side = 2 ** ((lo_count.bit_length() - 1) // 2)
    depth = lo_count // side
    plane = (hi_count // 2) * side
    hi, lo = lax.axis_index("hi"), lax.axis_index("lo")
    me = hi * lo_count + lo
    core = hi % 2
    spot = (hi // 2) * side + lo % side
    level = lo // side

    def place(core_to, level_to, spot_to):
        return ((spot_to // side) * 2 + core_to, level_to * side + spot_to % side)

    partner = place(1 - core, level, spot)
    peers_plane = [place(core, level, spot ^ j) for j in range(plane)]
    peers_depth = [place(core, level ^ r, spot) for r in range(depth)]

    loads = load_sem.shape[0]
    groups = count // LANES
    cuts = [c * groups // CUTS[-1] for c in CUTS]
    small = [pltpu.make_async_copy(signs_hbm, signs_ref, small_sem.at[0]),
             pltpu.make_async_copy(picks_hbm, picks_ref, small_sem.at[1]),
             pltpu.make_async_copy(rows_hbm, rows_ref, small_sem.at[2])]
    for copy in small:
        copy.start()

    def load(i):
        part = pl.ds(cuts[i] * LANES, (cuts[i + 1] - cuts[i]) * LANES)
        return pltpu.make_async_copy(panel_hbm.at[part], panel.at[part], load_sem.at[i])

    for i in range(loads):
        load(i).start()

    barrier = pltpu.get_barrier_semaphore()
    greet = [partner] + peers_plane[1:] + peers_depth[1:]
    for device in greet:
        pl.semaphore_signal(barrier, inc=1, device_id=device, device_id_type=MESH)

    left = lax.broadcasted_iota(jnp.int32, (LANES, 2 * LANES), 0)
    right = lax.broadcasted_iota(jnp.int32, (LANES, 2 * LANES), 1)
    had[...] = parity_sign(left & right & (LANES - 1)).astype(jnp.bfloat16)

    with jax.named_scope("small_waits"):
        for copy in small:
            copy.wait()

    ahead = 16
    more = 12

    def turn(line):
        return jnp.broadcast_to(line, (LANES, LANES)).T

    def factor(a):
        return turn(signs_ref[pl.ds(a, 1), :])

    with jax.named_scope("early_factors"):
        for a in range(ahead):
            wide[pl.ds(a * LANES, LANES), :] = factor(a)

    ready = ahead
    for i in range(loads):
        with jax.named_scope("load_wait"):
            load(i).wait()
        with jax.named_scope("products"):
            stop = cuts[i + 1]
            later = stop + more if i + 1 < loads else stop
            held = []
            extra = list(range(max(ready, stop), later))
            for pair in range(cuts[i] // 2, stop // 2):
                big, rest = [], []
                for q in range(2):
                    a = 2 * pair + q
                    rows = pl.ds(a * LANES, LANES)
                    by = wide[rows, :] if a < ready else factor(a)
                    block = panel[rows, :] * by
                    big.append(block.astype(jnp.bfloat16))
                    rest.append((block - big[q].astype(jnp.float32)).astype(jnp.bfloat16))
                both = jnp.concatenate(
                    [jnp.concatenate(big, axis=1), jnp.concatenate(rest, axis=1)], axis=0)
                done = jnp.dot(had[...], both, preferred_element_type=jnp.float32)
                x, y = done[:, :LANES], done[:, LANES:]
                two = [x + y, x - y]
                held.append(two)
                while len(held) > 1 and len(held[-1]) == len(held[-2]):
                    y, x = held.pop(), held.pop()
                    held.append([u + v for u, v in zip(x, y)] + [u - v for u, v in zip(x, y)])
                if len(held[0]) == FUSED:
                    for k, v in enumerate(held.pop()):
                        field[pl.ds((2 * pair + 2 - FUSED + k) * LANES, LANES), :] = v
                if extra and pair % 2 == 0:
                    for a in [extra.pop(0) for _ in range(min(2, len(extra)))]:
                        wide[pl.ds(a * LANES, LANES), :] = factor(a)
            for a in extra:
                wide[pl.ds(a * LANES, LANES), :] = factor(a)
            ready = later

    with jax.named_scope("butterflies"):
        steps = groups // FUSED
        tiles = FUSED * LANES // TILE
        lines = kept // LANES
        weights_ref[...] = parity_sign((picks_ref[...] // count) & me) * (1.0 / math.sqrt(total))

        @pl.loop(0, lines)
        def _(g):
            sgn[pl.ds(g * LANES, LANES), :] = turn(weights_ref[pl.ds(g, 1), :])
            for t in range(tiles // lines):
                p = g * (tiles // lines) + t
                rows = [pl.ds(b * FUSED * LANES + p * TILE, TILE) for b in range(steps)]
                parts = [field[r, :] for r in rows]
                half = 1
                while half < steps:
                    for b in range(steps):
                        if not b & half:
                            x, y = parts[b], parts[b + half]
                            parts[b], parts[b + half] = x + y, x - y
                    half *= 2
                for b in range(steps):
                    panel[rows[b], :] = parts[b]

    with jax.named_scope("barw"):
        pl.semaphore_wait(barrier, len(greet))

    def gather(dst, core_to, level_to):
        @pl.loop(0, plane)
        def _(j):
            hi_to, lo_to = place(core_to, level_to, spot ^ j)
            start = (hi_to * lo_count + lo_to) * share
            for s in range(share):
                row = rows_ref[start + s] & (count - 1)
                dst[pl.ds(j * share + s, 1), :] = panel[pl.ds(row, 1), :]
            part = pl.ds(j * share, share)
            dst[part, :] = dst[part, :] * sgn[pl.ds(start, share), :]

    def remote(src, dst, send, recv, device):
        return pltpu.make_async_remote_copy(
            src_ref=src, dst_ref=dst, send_sem=send, recv_sem=recv,
            device_id=device, device_id_type=MESH)

    levels = range(depth)
    sent_a, sent_b = {}, {}

    def send_pair(c):
        with jax.named_scope("gath1"):
            gather(terms.at[c], 1 - core, c)
        sent_a[c] = remote(terms.at[c], got_a.at[c], send_a.at[c], recv_a.at[c], partner)
        sent_a[c].start()
        if c:
            send_plane(c - 1)
        with jax.named_scope("gath2"):
            gather(mine.at[c], core, c)

    def send_plane(c):
        with jax.named_scope("waita"):
            sent_a[c].wait_recv()
        for j in list(range(1, plane)) + [0]:
            part = pl.ds(j * share, share)
            mine[c, part, :] = mine[c, part, :] + got_a[c, part, :]
            if j:
                sent_b[c, j] = remote(mine.at[c, part], got_b.at[c, part],
                                      send_b.at[c, j], recv_b.at[c, j], peers_plane[j])
                sent_b[c, j].start()

    def to_level(c):
        return remote(last.at[c], got_c.at[level], send_c.at[c], recv_c.at[level],
                      place(core, c, spot))

    def send_level(c):
        rows = mine[c, pl.ds(0, share), :]
        for j in range(1, plane):
            with jax.named_scope("waitb"):
                sent_b[c, j].wait_recv()
            rows = rows + got_b[c, pl.ds(j * share, share), :]
        last[c] = rows

        @pl.when(level != c)
        def _():
            to_level(c).start()

    for c in levels:
        send_pair(c)
    send_plane(depth - 1)
    for c in levels:
        send_level(c)
    result = last[level]
    for r in range(1, depth):
        other = level ^ r
        with jax.named_scope("waitc"):
            remote(last.at[other], got_c.at[other], send_c.at[other], recv_c.at[other],
               place(core, other, spot)).wait_recv()
        result = result + got_c[other]
    out_ref[...] = result
    for c in levels:
        sent_a[c].wait_send()
        for j in range(1, plane):
            sent_b[c, j].wait_send()

        @pl.when(level != c)
        def _():
            to_level(c).wait_send()


def body(panel, row_signs, sample_rows):
    count, width = panel.shape
    hi_count, lo_count = lax.axis_size("hi"), lax.axis_size("lo")
    kept = sample_rows.shape[0]
    share = kept // (hi_count * lo_count)
    side = 2 ** ((lo_count.bit_length() - 1) // 2)
    depth = lo_count // side
    plane = (hi_count // 2) * side
    loads = len(CUTS) - 1
    vmem = pl.BlockSpec(memory_space=pltpu.VMEM)
    dma = pltpu.SemaphoreType.DMA
    f32 = jnp.float32
    chunk = (depth, plane * share, width)
    return pl.pallas_call(
        functools.partial(kernel, hi_count, lo_count),
        out_shape=pltpu.VMEM((share, width), f32),
        in_specs=[pl.BlockSpec(memory_space=pltpu.HBM)] * 4,
        out_specs=vmem,
        scratch_shapes=[
            pltpu.VMEM((count, width), f32),
            pltpu.VMEM((count // LANES, LANES), f32),
            pltpu.SMEM((kept,), jnp.int32),
            pltpu.VMEM((kept // LANES, LANES), jnp.int32),
            pltpu.VMEM((count, width), f32),
            pltpu.VMEM((LANES, 2 * LANES), jnp.bfloat16),
            pltpu.VMEM((count, width), f32),
            pltpu.VMEM((kept // LANES, LANES), f32),
            pltpu.VMEM((kept, width), f32),
            pltpu.VMEM(chunk, f32),
            pltpu.VMEM(chunk, f32),
            pltpu.VMEM(chunk, f32),
            pltpu.VMEM(chunk, f32),
            pltpu.VMEM((depth, share, width), f32),
            pltpu.VMEM((depth, share, width), f32),
            dma((loads,)), dma((3,)),
            dma((depth,)), dma((depth,)),
            dma((depth, plane)), dma((depth, plane)),
            dma((depth,)), dma((depth,)),
        ],
        compiler_params=pltpu.CompilerParams(
            collective_id=0, has_side_effects=True, vmem_limit_bytes=60 * 2**20),
        cost_estimate=pl.CostEstimate(
            flops=2 * count * LOW * 2 * width, bytes_accessed=count * width * 4, transcendentals=0),
    )(panel, row_signs.reshape(count // LANES, LANES), sample_rows,
      sample_rows.reshape(kept // LANES, LANES))


def solution(mesh):
    placed = (P(("hi", "lo"), None), P(("hi", "lo"), None), P())
    return jax.shard_map(
        body, mesh=mesh, in_specs=placed, out_specs=P(("hi", "lo"), None), check_vma=False
    )
```

```python
import functools
import math

import jax
import jax.numpy as jnp
from jax import lax
from jax.experimental import pallas as pl
from jax.experimental.pallas import tpu as pltpu
from jax.sharding import PartitionSpec as P

MESH = pl.DeviceIdType.MESH
LOW = 256
LANES = 128
TILE = 8
FUSED = 8
CUTS = (0, 2, 5, 8)


def parity_sign(bits):
    shift = 16
    while shift:
        bits = bits ^ (bits >> shift)
        shift //= 2
    return (1 - 2 * (bits & 1)).astype(jnp.float32)


def kernel(hi_count, lo_count, panel_hbm, signs_hbm, rows_hbm, picks_hbm, out_ref,
           panel, signs_ref, rows_ref, picks_ref, field, had, wide, sgn, terms, mine, got_a, got_b, got_c, last,
           first, got_first, head, got_head,
           load_sem, small_sem, send_a, recv_a, send_b, recv_b, send_c, recv_c,
           send_f, recv_f, send_h, recv_h):
    count = panel.shape[0]
    share = out_ref.shape[0]
    kept = rows_ref.shape[0]
    total = count * hi_count * lo_count
    side = 2 ** ((lo_count.bit_length() - 1) // 2)
    depth = lo_count // side
    plane = (hi_count // 2) * side
    hi, lo = lax.axis_index("hi"), lax.axis_index("lo")
    me = hi * lo_count + lo
    core = hi % 2
    spot = (hi // 2) * side + lo % side
    level = lo // side

    def place(core_to, level_to, spot_to):
        return ((spot_to // side) * 2 + core_to, level_to * side + spot_to % side)

    partner = place(1 - core, level, spot)
    peers_plane = [place(core, level, spot ^ j) for j in range(plane)]
    peers_depth = [place(core, level ^ r, spot) for r in range(depth)]

    loads = load_sem.shape[0]
    groups = count // LANES
    cuts = [c * groups // CUTS[-1] for c in CUTS]
    small = [pltpu.make_async_copy(signs_hbm, signs_ref, small_sem.at[0]),
             pltpu.make_async_copy(picks_hbm, picks_ref, small_sem.at[1]),
             pltpu.make_async_copy(rows_hbm, rows_ref, small_sem.at[2])]
    for copy in small:
        copy.start()

    def load(i):
        part = pl.ds(cuts[i] * LANES, (cuts[i + 1] - cuts[i]) * LANES)
        return pltpu.make_async_copy(panel_hbm.at[part], panel.at[part], load_sem.at[i])

    for i in range(loads):
        load(i).start()

    barrier = pltpu.get_barrier_semaphore()
    greet = [partner] + peers_plane[1:] + peers_depth[1:]
    greet += [place(1 - core, level, spot ^ j) for j in range(1, plane)]
    for device in greet:
        pl.semaphore_signal(barrier, inc=1, device_id=device, device_id_type=MESH)

    left = lax.broadcasted_iota(jnp.int32, (LANES, 2 * LANES), 0)
    right = lax.broadcasted_iota(jnp.int32, (LANES, 2 * LANES), 1)
    had[...] = parity_sign(left & right & (LANES - 1)).astype(jnp.bfloat16)

    with jax.named_scope("small_waits"):
        for copy in small:
            copy.wait()

    ahead = 8
    more = 8

    def turn(line):
        return jnp.broadcast_to(line, (LANES, LANES)).T

    def factor(a):
        return turn(signs_ref[pl.ds(a, 1), :])

    with jax.named_scope("early_factors"):
        for a in range(ahead):
            wide[pl.ds(a * LANES, LANES), :] = factor(a)

    ready = ahead
    for i in range(loads):
        with jax.named_scope("load_wait"):
            load(i).wait()
        with jax.named_scope("products"):
            stop = cuts[i + 1]
            later = stop + more if i + 1 < loads else stop
            held = []
            lines = []
            if i == loads - 1:
                weight = parity_sign((picks_ref[...] // count) & me) * (1.0 / math.sqrt(total))
                lines = list(range(kept // LANES))
            extra = list(range(max(ready, stop), later))
            for pair in range(cuts[i] // 2, stop // 2):
                big, rest = [], []
                for q in range(2):
                    a = 2 * pair + q
                    rows = pl.ds(a * LANES, LANES)
                    by = wide[rows, :] if a < ready else factor(a)
                    block = panel[rows, :] * by
                    big.append(block.astype(jnp.bfloat16))
                    rest.append((block - big[q].astype(jnp.float32)).astype(jnp.bfloat16))
                both = jnp.concatenate(
                    [jnp.concatenate(big, axis=1), jnp.concatenate(rest, axis=1)], axis=0)
                done = jnp.dot(had[...], both, preferred_element_type=jnp.float32)
                x, y = done[:, :LANES], done[:, LANES:]
                two = [x + y, x - y]
                held.append(two)
                while len(held) > 1 and len(held[-1]) == len(held[-2]):
                    y, x = held.pop(), held.pop()
                    held.append([u + v for u, v in zip(x, y)] + [u - v for u, v in zip(x, y)])
                if len(held[0]) == FUSED:
                    for k, v in enumerate(held.pop()):
                        field[pl.ds((2 * pair + 2 - FUSED + k) * LANES, LANES), :] = v
                if lines:
                    g = lines.pop(0)
                    sgn[pl.ds(g * LANES, LANES), :] = turn(weight[g:g + 1, :])
                if extra and pair % 2 == 0:
                    for a in [extra.pop(0) for _ in range(min(2, len(extra)))]:
                        wide[pl.ds(a * LANES, LANES), :] = factor(a)
            for g in lines:
                sgn[pl.ds(g * LANES, LANES), :] = turn(weight[g:g + 1, :])
            for a in extra:
                wide[pl.ds(a * LANES, LANES), :] = factor(a)
            ready = later

    with jax.named_scope("butterflies"):
        steps = groups // FUSED
        tiles = FUSED * LANES // TILE
        lines = 8

        @pl.loop(0, lines)
        def _(g):
            for t in range(tiles // lines):
                p = g * (tiles // lines) + t
                rows = [pl.ds(b * FUSED * LANES + p * TILE, TILE) for b in range(steps)]
                parts = [field[r, :] for r in rows]
                half = 1
                while half < steps:
                    for b in range(steps):
                        if not b & half:
                            x, y = parts[b], parts[b + half]
                            parts[b], parts[b + half] = x + y, x - y
                    half *= 2
                for b in range(steps):
                    panel[rows[b], :] = parts[b]

    with jax.named_scope("entry_wait"):
        pl.semaphore_wait(barrier, len(greet))

    def gather(dst, base, core_to, level_to, spot_to):
        hi_to, lo_to = place(core_to, level_to, spot_to)
        start = (hi_to * lo_count + lo_to) * share
        for s in range(share):
            row = rows_ref[start + s] & (count - 1)
            dst[pl.ds(base + s, 1), :] = panel[pl.ds(row, 1), :]
        part = pl.ds(base, share)
        dst[part, :] = dst[part, :] * sgn[pl.ds(start, share), :]

    def gather_level(dst, core_to, level_to):
        @pl.loop(0, plane)
        def _(j):
            if level_to:
                gather(dst, j * share, core_to, level_to, spot ^ j)
            else:
                @pl.when(spot != j)
                def _():
                    gather(dst, j * share, core_to, level_to, spot ^ j)

    def remote(src, dst, send, recv, device):
        return pltpu.make_async_remote_copy(
            src_ref=src, dst_ref=dst, send_sem=send, recv_sem=recv,
            device_id=device, device_id_type=MESH)

    levels = range(depth)

    def to_first(k):
        return remote(first.at[k], got_first.at[spot * 2 + core], send_f.at[k], recv_f.at[spot * 2 + core],
                      place(k, level, 0))

    def to_partner(c):
        return remote(terms.at[c], got_a.at[c], send_a.at[c], recv_a.at[c], partner)

    def to_plane(c, j):
        part = pl.ds(j * share, share)
        return remote(mine.at[c, part], got_b.at[c, part], send_b.at[c, j], recv_b.at[c, j], peers_plane[j])

    def to_level(c):
        return remote(last.at[c], got_c.at[level], send_c.at[c], recv_c.at[level], place(core, c, spot))

    def to_head():
        return remote(head, got_head.at[level], send_h.at[0], recv_h.at[level], place(core, 0, 0))

    def guarded(condition, action):
        pl.when(condition)(action)

    def send_first():
        for k in range(2):
            gather(first.at[k], 0, k, 0, 0)
            guarded((spot != 0) | (core != k), lambda k=k: to_first(k).start())

    def send_pair(c):
        gather_level(terms.at[c], 1 - core, c)
        to_partner(c).start()

    def send_plane(c):
        gather_level(mine.at[c], core, c)
        with jax.named_scope("partner_wait"):
            to_partner(c).wait_recv()

        def part_sum(j):
            part = pl.ds(j * share, share)
            mine[c, part, :] = mine[c, part, :] + got_a[c, part, :]
            if j:
                to_plane(c, j).start()

        for j in list(range(1, plane)) + [0]:
            if c:
                part_sum(j)
            else:
                guarded(spot != j, lambda j=j: part_sum(j))

    def sum_first():
        total = first[core]
        with jax.named_scope("first_wait"):
            for i in range(2 * plane):
                def arrived(i=i):
                    remote(first.at[0], got_first.at[i], send_f.at[0], recv_f.at[i], partner).wait_recv()
                if i < 2:
                    guarded(core != i, arrived)
                else:
                    arrived()
        total = total + got_first[1 - core]
        for i in range(2, 2 * plane):
            total = total + got_first[i]
        head[...] = total
        guarded(level != 0, lambda: to_head().start())

    def send_level(c):
        rows = mine[c, pl.ds(0, share), :]
        for j in range(1, plane):
            with jax.named_scope("plane_wait"):
                to_plane(c, j).wait_recv()
            rows = rows + got_b[c, pl.ds(j * share, share), :]
        last[c] = rows
        guarded(level != c, lambda: to_level(c).start())

    with jax.named_scope("first_rows"):
        send_first()
    lead = min(3, depth)
    for c in range(lead):
        with jax.named_scope("gather_partner"):
            send_pair(c)
    for c in levels:
        with jax.named_scope("gather_own"):
            send_plane(c)
        if c + lead < depth:
            send_pair(c + lead)

    guarded(spot == 0, sum_first)
    guarded(spot != 0, lambda: send_level(0))
    for c in levels[1:]:
        send_level(c)

    is_first = (spot == 0) & (level == 0)

    @pl.when(is_first)
    def _():
        result = head[...]
        for other in range(1, depth):
            with jax.named_scope("head_wait"):
                remote(head, got_head.at[other], send_h.at[0], recv_h.at[other], partner).wait_recv()
            result = result + got_head[other]
        out_ref[...] = result

    @pl.when(jnp.logical_not(is_first))
    def _():
        result = last[level]
        for r in range(1, depth):
            other = level ^ r
            with jax.named_scope("level_wait"):
                remote(last.at[other], got_c.at[other], send_c.at[other], recv_c.at[other],
                       place(core, other, spot)).wait_recv()
            result = result + got_c[other]
        out_ref[...] = result

    for k in range(2):
        guarded((spot != 0) | (core != k), lambda k=k: to_first(k).wait_send())
    guarded((spot == 0) & (level != 0), lambda: to_head().wait_send())
    for c in levels:
        to_partner(c).wait_send()
        for j in range(1, plane):
            if c:
                to_plane(c, j).wait_send()
            else:
                guarded(spot != j, lambda j=j: to_plane(0, j).wait_send())
        there = level != c
        guarded(there if c else there & (spot != 0), lambda c=c: to_level(c).wait_send())


def body(panel, row_signs, sample_rows):
    count, width = panel.shape
    hi_count, lo_count = lax.axis_size("hi"), lax.axis_size("lo")
    kept = sample_rows.shape[0]
    share = kept // (hi_count * lo_count)
    side = 2 ** ((lo_count.bit_length() - 1) // 2)
    depth = lo_count // side
    plane = (hi_count // 2) * side
    loads = len(CUTS) - 1
    vmem = pl.BlockSpec(memory_space=pltpu.VMEM)
    dma = pltpu.SemaphoreType.DMA
    f32 = jnp.float32
    chunk = (depth, plane * share, width)
    return pl.pallas_call(
        functools.partial(kernel, hi_count, lo_count),
        out_shape=pltpu.VMEM((share, width), f32),
        in_specs=[pl.BlockSpec(memory_space=pltpu.HBM)] * 4,
        out_specs=vmem,
        scratch_shapes=[
            pltpu.VMEM((count, width), f32),
            pltpu.VMEM((count // LANES, LANES), f32),
            pltpu.SMEM((kept,), jnp.int32),
            pltpu.VMEM((kept // LANES, LANES), jnp.int32),
            pltpu.VMEM((count, width), f32),
            pltpu.VMEM((LANES, 2 * LANES), jnp.bfloat16),
            pltpu.VMEM((count, width), f32),
            pltpu.VMEM((kept, width), f32),
            pltpu.VMEM(chunk, f32),
            pltpu.VMEM(chunk, f32),
            pltpu.VMEM(chunk, f32),
            pltpu.VMEM(chunk, f32),
            pltpu.VMEM((depth, share, width), f32),
            pltpu.VMEM((depth, share, width), f32),
            pltpu.VMEM((2, share, width), f32),
            pltpu.VMEM((2 * plane, share, width), f32),
            pltpu.VMEM((share, width), f32),
            pltpu.VMEM((depth, share, width), f32),
            dma((loads,)), dma((3,)),
            dma((depth,)), dma((depth,)),
            dma((depth, plane)), dma((depth, plane)),
            dma((depth,)), dma((depth,)),
            dma((2,)), dma((2 * plane,)),
            dma((1,)), dma((depth,)),
        ],
        compiler_params=pltpu.CompilerParams(
            collective_id=0, has_side_effects=True, vmem_limit_bytes=60 * 2**20),
        cost_estimate=pl.CostEstimate(
            flops=2 * count * LOW * 2 * width, bytes_accessed=count * width * 4, transcendentals=0),
    )(panel, row_signs.reshape(count // LANES, LANES), sample_rows,
      sample_rows.reshape(kept // LANES, LANES))


def solution(mesh):
    placed = (P(("hi", "lo"), None), P(("hi", "lo"), None), P())
    return jax.shard_map(
        body, mesh=mesh, in_specs=placed, out_specs=P(("hi", "lo"), None), check_vma=False
    )
```

```python
import functools
import math

import jax
import jax.numpy as jnp
from jax import lax
from jax.experimental import pallas as pl
from jax.experimental.pallas import tpu as pltpu
from jax.sharding import PartitionSpec as P

MESH = pl.DeviceIdType.MESH
LOW = 256
LANES = 128
TILE = 8
FUSED = 8
CUTS = (0, 2, 5, 8)


def parity_sign(bits):
    shift = 16
    while shift:
        bits = bits ^ (bits >> shift)
        shift //= 2
    return (1 - 2 * (bits & 1)).astype(jnp.float32)


def kernel(hi_count, lo_count, panel_hbm, signs_hbm, rows_hbm, picks_hbm, out_ref,
           panel, signs_ref, rows_ref, picks_ref, field, had, wide, sgn, terms, mine, got_a, got_b, got_c, last,
           first, got_first, head, got_head,
           load_sem, small_sem, send_a, recv_a, send_b, recv_b, send_c, recv_c,
           send_f, recv_f, send_h, recv_h):
    count = panel.shape[0]
    share = out_ref.shape[0]
    kept = rows_ref.shape[0]
    total = count * hi_count * lo_count
    side = 2 ** ((lo_count.bit_length() - 1) // 2)
    depth = lo_count // side
    plane = (hi_count // 2) * side
    hi, lo = lax.axis_index("hi"), lax.axis_index("lo")
    me = hi * lo_count + lo
    core = hi % 2
    spot = (hi // 2) * side + lo % side
    level = lo // side

    def place(core_to, level_to, spot_to):
        return ((spot_to // side) * 2 + core_to, level_to * side + spot_to % side)

    partner = place(1 - core, level, spot)
    peers_plane = [place(core, level, spot ^ j) for j in range(plane)]
    peers_depth = [place(core, level ^ r, spot) for r in range(depth)]

    loads = load_sem.shape[0]
    groups = count // LANES
    cuts = [c * groups // CUTS[-1] for c in CUTS]
    small = [pltpu.make_async_copy(signs_hbm, signs_ref, small_sem.at[0]),
             pltpu.make_async_copy(picks_hbm, picks_ref, small_sem.at[1]),
             pltpu.make_async_copy(rows_hbm, rows_ref, small_sem.at[2])]
    for copy in small:
        copy.start()

    def load(i):
        part = pl.ds(cuts[i] * LANES, (cuts[i + 1] - cuts[i]) * LANES)
        return pltpu.make_async_copy(panel_hbm.at[part], panel.at[part], load_sem.at[i])

    for i in range(loads):
        load(i).start()

    barrier = pltpu.get_barrier_semaphore()
    greet = [partner] + peers_plane[1:] + peers_depth[1:]
    greet += [place(1 - core, level, spot ^ j) for j in range(1, plane)]
    greet += [place(1 - core, level ^ r, spot) for r in range(1, depth)]
    for device in greet:
        pl.semaphore_signal(barrier, inc=1, device_id=device, device_id_type=MESH)

    left = lax.broadcasted_iota(jnp.int32, (LANES, 2 * LANES), 0)
    right = lax.broadcasted_iota(jnp.int32, (LANES, 2 * LANES), 1)
    had[...] = parity_sign(left & right & (LANES - 1)).astype(jnp.bfloat16)

    with jax.named_scope("small_waits"):
        for copy in small:
            copy.wait()

    ahead = 8
    more = 8

    def turn(line):
        return jnp.broadcast_to(line, (LANES, LANES)).T

    def factor(a):
        return turn(signs_ref[pl.ds(a, 1), :])

    with jax.named_scope("early_factors"):
        for a in range(ahead):
            wide[pl.ds(a * LANES, LANES), :] = factor(a)

    ready = ahead
    for i in range(loads):
        with jax.named_scope("load_wait"):
            load(i).wait()
        with jax.named_scope("products"):
            stop = cuts[i + 1]
            later = stop + more if i + 1 < loads else stop
            held = []
            lines = []
            if i == loads - 1:
                weight = parity_sign((picks_ref[...] // count) & me) * (1.0 / math.sqrt(total))
                lines = list(range(kept // LANES))
            extra = list(range(max(ready, stop), later))
            for pair in range(cuts[i] // 2, stop // 2):
                big, rest = [], []
                for q in range(2):
                    a = 2 * pair + q
                    rows = pl.ds(a * LANES, LANES)
                    by = wide[rows, :] if a < ready else factor(a)
                    block = panel[rows, :] * by
                    big.append(block.astype(jnp.bfloat16))
                    rest.append((block - big[q].astype(jnp.float32)).astype(jnp.bfloat16))
                both = jnp.concatenate(
                    [jnp.concatenate(big, axis=1), jnp.concatenate(rest, axis=1)], axis=0)
                done = jnp.dot(had[...], both, preferred_element_type=jnp.float32)
                x, y = done[:, :LANES], done[:, LANES:]
                two = [x + y, x - y]
                held.append(two)
                while len(held) > 1 and len(held[-1]) == len(held[-2]):
                    y, x = held.pop(), held.pop()
                    held.append([u + v for u, v in zip(x, y)] + [u - v for u, v in zip(x, y)])
                if len(held[0]) == FUSED:
                    for k, v in enumerate(held.pop()):
                        field[pl.ds((2 * pair + 2 - FUSED + k) * LANES, LANES), :] = v
                if lines:
                    g = lines.pop(0)
                    sgn[pl.ds(g * LANES, LANES), :] = turn(weight[g:g + 1, :])
                if extra and pair % 2 == 0:
                    for a in [extra.pop(0) for _ in range(min(2, len(extra)))]:
                        wide[pl.ds(a * LANES, LANES), :] = factor(a)
            for g in lines:
                sgn[pl.ds(g * LANES, LANES), :] = turn(weight[g:g + 1, :])
            for a in extra:
                wide[pl.ds(a * LANES, LANES), :] = factor(a)
            ready = later

    with jax.named_scope("butterflies"):
        steps = groups // FUSED
        tiles = FUSED * LANES // TILE
        lines = 8

        @pl.loop(0, lines)
        def _(g):
            for t in range(tiles // lines):
                p = g * (tiles // lines) + t
                rows = [pl.ds(b * FUSED * LANES + p * TILE, TILE) for b in range(steps)]
                parts = [field[r, :] for r in rows]
                half = 1
                while half < steps:
                    for b in range(steps):
                        if not b & half:
                            x, y = parts[b], parts[b + half]
                            parts[b], parts[b + half] = x + y, x - y
                    half *= 2
                for b in range(steps):
                    panel[rows[b], :] = parts[b]

    with jax.named_scope("entry_wait"):
        pl.semaphore_wait(barrier, len(greet))

    def gather(dst, base, core_to, level_to, spot_to):
        hi_to, lo_to = place(core_to, level_to, spot_to)
        start = (hi_to * lo_count + lo_to) * share
        for s in range(share):
            row = rows_ref[start + s] & (count - 1)
            dst[pl.ds(base + s, 1), :] = panel[pl.ds(row, 1), :]
        part = pl.ds(base, share)
        dst[part, :] = dst[part, :] * sgn[pl.ds(start, share), :]

    def gather_level(dst, core_to, level_to):
        @pl.loop(0, plane)
        def _(j):
            if level_to:
                gather(dst, j * share, core_to, level_to, spot ^ j)
            else:
                @pl.when(spot != j)
                def _():
                    gather(dst, j * share, core_to, level_to, spot ^ j)

    def remote(src, dst, send, recv, device):
        return pltpu.make_async_remote_copy(
            src_ref=src, dst_ref=dst, send_sem=send, recv_sem=recv,
            device_id=device, device_id_type=MESH)

    levels = range(depth)

    reducer = (core == 1) & (spot == 0)
    slot = (spot * 2 + core) ^ 1

    def to_first():
        return remote(first, got_first.at[slot], send_f.at[0], recv_f.at[0], place(1, level, 0))

    def to_head(k):
        return remote(head.at[k], got_head.at[level], send_h.at[0], recv_h.at[0], place(k, 0, 0))

    def to_partner(c):
        return remote(terms.at[c], got_a.at[c], send_a.at[0], recv_a.at[c], partner)

    def to_plane(c, j):
        part = pl.ds(j * share, share)
        return remote(mine.at[c, part], got_b.at[c, part], send_b.at[min(c, 1)], recv_b.at[c], peers_plane[j])

    def to_level(c):
        return remote(last.at[c], got_c.at[level], send_c.at[0], recv_c.at[0], place(core, c, spot))

    def received(ref, recv):
        remote(ref, ref, send_f.at[0], recv, partner).wait_recv()

    def sent(ref, send):
        remote(ref, ref, send, recv_f.at[0], partner).wait_send()

    def guarded(condition, action):
        pl.when(condition)(action)

    def send_first():
        for k in range(2):
            gather(first.at[k], 0, k, 0, 0)
        guarded(jnp.logical_not(reducer), lambda: to_first().start())

    def send_pair(c):
        gather_level(terms.at[c], 1 - core, c)
        to_partner(c).start()

    def send_plane(c):
        gather_level(mine.at[c], core, c)
        with jax.named_scope("partner_wait"):
            to_partner(c).wait_recv()

        def part_sum(j):
            part = pl.ds(j * share, share)
            mine[c, part, :] = mine[c, part, :] + got_a[c, part, :]
            if j:
                to_plane(c, j).start()

        for j in list(range(1, plane)) + [0]:
            if c:
                part_sum(j)
            else:
                guarded(spot != j, lambda j=j: part_sum(j))

    def sum_first():
        with jax.named_scope("first_wait"):
            received(got_first.at[pl.ds(1, 2 * plane - 1)], recv_f.at[0])
        for k in range(2):
            total = first[k]
            for i in range(1, 2 * plane):
                total = total + got_first[i, k]
            head[k] = total
            if k:
                guarded(level != 0, lambda: to_head(1).start())
            else:
                to_head(0).start()

    def send_level(c):
        with jax.named_scope("plane_wait"):
            received(got_b.at[c, pl.ds(share, (plane - 1) * share)], recv_b.at[c])
        rows = mine[c, pl.ds(0, share), :]
        for j in range(1, plane):
            rows = rows + got_b[c, pl.ds(j * share, share), :]
        last[c] = rows
        guarded(level != c, lambda: to_level(c).start())

    with jax.named_scope("first_rows"):
        send_first()
    lead = min(3, depth)
    for c in range(lead):
        with jax.named_scope("gather_partner"):
            send_pair(c)
    for c in levels:
        with jax.named_scope("gather_own"):
            send_plane(c)
        if c + lead < depth:
            send_pair(c + lead)

    guarded(reducer, sum_first)
    guarded(spot != 0, lambda: send_level(0))
    for c in levels[1:]:
        send_level(c)

    is_first = (spot == 0) & (level == 0)
    others = pl.ds(1, depth - 1)

    @pl.when(is_first & (core == 0))
    def _():
        with jax.named_scope("head_wait"):
            received(got_head, recv_h.at[0])
        result = got_head[0]
        for other in range(1, depth):
            result = result + got_head[other]
        out_ref[...] = result

    @pl.when(is_first & (core == 1))
    def _():
        with jax.named_scope("head_wait"):
            received(got_head.at[others], recv_h.at[0])
        result = head[1]
        for other in range(1, depth):
            result = result + got_head[other]
        out_ref[...] = result

    @pl.when(jnp.logical_not(is_first))
    def _():
        with jax.named_scope("level_wait"):
            received(got_c.at[others], recv_c.at[0])
        result = last[level]
        for r in range(1, depth):
            result = result + got_c[level ^ r]
        out_ref[...] = result

    guarded(jnp.logical_not(reducer), lambda: to_first().wait_send())
    guarded(reducer & (level != 0), lambda: sent(head, send_h.at[0]))
    guarded(reducer & (level == 0), lambda: to_head(0).wait_send())
    sent(terms, send_a.at[0])
    sent(mine.at[others, pl.ds(share, (plane - 1) * share)], send_b.at[1])
    guarded(spot == 0, lambda: sent(mine.at[0, pl.ds(share, (plane - 1) * share)], send_b.at[0]))
    guarded(spot != 0, lambda: sent(mine.at[0, pl.ds(share, (plane - 2) * share)], send_b.at[0]))
    fewer = (spot == 0) & (level != 0)
    guarded(fewer, lambda: sent(last.at[pl.ds(0, depth - 2)], send_c.at[0]))
    guarded(jnp.logical_not(fewer), lambda: sent(last.at[pl.ds(0, depth - 1)], send_c.at[0]))


def body(panel, row_signs, sample_rows):
    count, width = panel.shape
    hi_count, lo_count = lax.axis_size("hi"), lax.axis_size("lo")
    kept = sample_rows.shape[0]
    share = kept // (hi_count * lo_count)
    side = 2 ** ((lo_count.bit_length() - 1) // 2)
    depth = lo_count // side
    plane = (hi_count // 2) * side
    loads = len(CUTS) - 1
    vmem = pl.BlockSpec(memory_space=pltpu.VMEM)
    dma = pltpu.SemaphoreType.DMA
    f32 = jnp.float32
    chunk = (depth, plane * share, width)
    return pl.pallas_call(
        functools.partial(kernel, hi_count, lo_count),
        out_shape=pltpu.VMEM((share, width), f32),
        in_specs=[pl.BlockSpec(memory_space=pltpu.HBM)] * 4,
        out_specs=vmem,
        scratch_shapes=[
            pltpu.VMEM((count, width), f32),
            pltpu.VMEM((count // LANES, LANES), f32),
            pltpu.SMEM((kept,), jnp.int32),
            pltpu.VMEM((kept // LANES, LANES), jnp.int32),
            pltpu.VMEM((count, width), f32),
            pltpu.VMEM((LANES, 2 * LANES), jnp.bfloat16),
            pltpu.VMEM((count, width), f32),
            pltpu.VMEM((kept, width), f32),
            pltpu.VMEM(chunk, f32),
            pltpu.VMEM(chunk, f32),
            pltpu.VMEM(chunk, f32),
            pltpu.VMEM(chunk, f32),
            pltpu.VMEM((depth, share, width), f32),
            pltpu.VMEM((depth, share, width), f32),
            pltpu.VMEM((2, share, width), f32),
            pltpu.VMEM((2 * plane, 2, share, width), f32),
            pltpu.VMEM((2, share, width), f32),
            pltpu.VMEM((depth, share, width), f32),
            dma((loads,)), dma((3,)),
            dma((1,)), dma((depth,)),
            dma((2,)), dma((depth,)),
            dma((1,)), dma((1,)),
            dma((1,)), dma((1,)),
            dma((1,)), dma((1,)),
        ],
        compiler_params=pltpu.CompilerParams(
            collective_id=0, has_side_effects=True, vmem_limit_bytes=60 * 2**20),
        cost_estimate=pl.CostEstimate(
            flops=2 * count * LOW * 2 * width, bytes_accessed=count * width * 4, transcendentals=0),
    )(panel, row_signs.reshape(count // LANES, LANES), sample_rows,
      sample_rows.reshape(kept // LANES, LANES))


def solution(mesh):
    placed = (P(("hi", "lo"), None), P(("hi", "lo"), None), P())
    return jax.shard_map(
        body, mesh=mesh, in_specs=placed, out_specs=P(("hi", "lo"), None), check_vma=False
    )
```

```python
import functools
import math

import jax
import jax.numpy as jnp
from jax import lax
from jax.experimental import pallas as pl
from jax.experimental.pallas import tpu as pltpu
from jax.sharding import PartitionSpec as P

MESH = pl.DeviceIdType.MESH
LOW = 256
LANES = 128
TILE = 8
FUSED = 8
CUTS = (0, 2, 5, 8)


def parity_sign(bits):
    shift = 16
    while shift:
        bits = bits ^ (bits >> shift)
        shift //= 2
    return (1 - 2 * (bits & 1)).astype(jnp.float32)


def kernel(hi_count, lo_count, panel_hbm, signs_hbm, rows_hbm, picks_hbm, out_ref,
           panel, signs_ref, rows_ref, picks_ref, field, had, wide, sgn, terms, mine, got_a, got_b, got_c, last,
           first, got_first, head, got_head,
           load_sem, small_sem, send_a, recv_a, send_b, recv_b, send_c, recv_c,
           send_f, recv_f, send_h, recv_h):
    count = panel.shape[0]
    share = out_ref.shape[0]
    kept = rows_ref.shape[0]
    total = count * hi_count * lo_count
    side = 2 ** ((lo_count.bit_length() - 1) // 2)
    depth = lo_count // side
    plane = (hi_count // 2) * side
    hi, lo = lax.axis_index("hi"), lax.axis_index("lo")
    me = hi * lo_count + lo
    core = hi % 2
    spot = (hi // 2) * side + lo % side
    level = lo // side

    def place(core_to, level_to, spot_to):
        return ((spot_to // side) * 2 + core_to, level_to * side + spot_to % side)

    partner = place(1 - core, level, spot)
    peers_plane = [place(core, level, spot ^ j) for j in range(plane)]
    peers_depth = [place(core, level ^ r, spot) for r in range(depth)]

    loads = load_sem.shape[0]
    groups = count // LANES
    cuts = [c * groups // CUTS[-1] for c in CUTS]
    small = [pltpu.make_async_copy(signs_hbm, signs_ref, small_sem.at[0]),
             pltpu.make_async_copy(picks_hbm, picks_ref, small_sem.at[1]),
             pltpu.make_async_copy(rows_hbm, rows_ref, small_sem.at[2])]
    for copy in small:
        copy.start()

    def load(i):
        part = pl.ds(cuts[i] * LANES, (cuts[i + 1] - cuts[i]) * LANES)
        return pltpu.make_async_copy(panel_hbm.at[part], panel.at[part], load_sem.at[i])

    for i in range(loads):
        load(i).start()

    barrier = pltpu.get_barrier_semaphore()
    greet = [partner] + peers_plane[1:] + peers_depth[1:]
    greet += [place(1 - core, level, spot ^ j) for j in range(1, plane)]
    greet += [place(1 - core, level ^ r, spot) for r in range(1, depth)]
    for device in greet:
        pl.semaphore_signal(barrier, inc=1, device_id=device, device_id_type=MESH)

    left = lax.broadcasted_iota(jnp.int32, (LANES, 2 * LANES), 0)
    right = lax.broadcasted_iota(jnp.int32, (LANES, 2 * LANES), 1)
    had[...] = parity_sign(left & right & (LANES - 1)).astype(jnp.bfloat16)

    with jax.named_scope("small_waits"):
        for copy in small:
            copy.wait()

    ahead = 8
    more = 8

    def turn(line):
        return jnp.broadcast_to(line, (LANES, LANES)).T

    def factor(a):
        return turn(signs_ref[pl.ds(a, 1), :])

    with jax.named_scope("early_factors"):
        for a in range(ahead):
            wide[pl.ds(a * LANES, LANES), :] = factor(a)

    ready = ahead
    for i in range(loads):
        with jax.named_scope("load_wait"):
            load(i).wait()
        with jax.named_scope("products"):
            stop = cuts[i + 1]
            later = stop + more if i + 1 < loads else stop
            held = []
            lines = []
            if i == loads - 1:
                weight = parity_sign((picks_ref[...] // count) & me) * (1.0 / math.sqrt(total))
                lines = list(range(kept // LANES))
            extra = list(range(max(ready, stop), later))
            for pair in range(cuts[i] // 2, stop // 2):
                big, rest = [], []
                for q in range(2):
                    a = 2 * pair + q
                    rows = pl.ds(a * LANES, LANES)
                    by = wide[rows, :] if a < ready else factor(a)
                    block = panel[rows, :] * by
                    big.append(block.astype(jnp.bfloat16))
                    rest.append((block - big[q].astype(jnp.float32)).astype(jnp.bfloat16))
                both = jnp.concatenate(
                    [jnp.concatenate(big, axis=1), jnp.concatenate(rest, axis=1)], axis=0)
                done = jnp.dot(had[...], both, preferred_element_type=jnp.float32)
                x, y = done[:, :LANES], done[:, LANES:]
                two = [x + y, x - y]
                held.append(two)
                while len(held) > 1 and len(held[-1]) == len(held[-2]):
                    y, x = held.pop(), held.pop()
                    held.append([u + v for u, v in zip(x, y)] + [u - v for u, v in zip(x, y)])
                if len(held[0]) == FUSED:
                    for k, v in enumerate(held.pop()):
                        field[pl.ds((2 * pair + 2 - FUSED + k) * LANES, LANES), :] = v
                if lines:
                    g = lines.pop(0)
                    sgn[pl.ds(g * LANES, LANES), :] = turn(weight[g:g + 1, :])
                if extra and pair % 2 == 0:
                    for a in [extra.pop(0) for _ in range(min(2, len(extra)))]:
                        wide[pl.ds(a * LANES, LANES), :] = factor(a)
            for g in lines:
                sgn[pl.ds(g * LANES, LANES), :] = turn(weight[g:g + 1, :])
            for a in extra:
                wide[pl.ds(a * LANES, LANES), :] = factor(a)
            ready = later

    with jax.named_scope("butterflies"):
        steps = groups // FUSED
        tiles = FUSED * LANES // TILE
        lines = 8

        @pl.loop(0, lines)
        def _(g):
            for t in range(tiles // lines):
                p = g * (tiles // lines) + t
                rows = [pl.ds(b * FUSED * LANES + p * TILE, TILE) for b in range(steps)]
                parts = [field[r, :] for r in rows]
                half = 1
                while half < steps:
                    for b in range(steps):
                        if not b & half:
                            x, y = parts[b], parts[b + half]
                            parts[b], parts[b + half] = x + y, x - y
                    half *= 2
                for b in range(steps):
                    panel[rows[b], :] = parts[b]

    with jax.named_scope("entry_wait"):
        pl.semaphore_wait(barrier, len(greet))

    def gather(dst, base, core_to, level_to, spot_to):
        hi_to, lo_to = place(core_to, level_to, spot_to)
        start = (hi_to * lo_count + lo_to) * share
        for s in range(share):
            row = rows_ref[start + s] & (count - 1)
            dst[pl.ds(base + s, 1), :] = panel[pl.ds(row, 1), :]
        part = pl.ds(base, share)
        dst[part, :] = dst[part, :] * sgn[pl.ds(start, share), :]

    def gather_level(dst, core_to, level_to):
        @pl.loop(0, plane)
        def _(j):
            if level_to:
                gather(dst, j * share, core_to, level_to, spot ^ j)
            else:
                @pl.when(spot != j)
                def _():
                    gather(dst, j * share, core_to, level_to, spot ^ j)

    def remote(src, dst, send, recv, device):
        return pltpu.make_async_remote_copy(
            src_ref=src, dst_ref=dst, send_sem=send, recv_sem=recv,
            device_id=device, device_id_type=MESH)

    levels = range(depth)

    reducer = (core == 1) & (spot == 0)
    slot = (spot * 2 + core) ^ 1

    def to_first(k):
        return remote(first.at[k], got_first.at[k, slot], send_f.at[0], recv_f.at[k], place(1, level, 0))

    def to_head(k):
        return remote(head.at[k], got_head.at[level], send_h.at[0], recv_h.at[0], place(k, 0, 0))

    def to_partner(c):
        return remote(terms.at[c], got_a.at[c], send_a.at[0], recv_a.at[c], partner)

    def to_plane(c, j):
        part = pl.ds(j * share, share)
        return remote(mine.at[c, part], got_b.at[core, c, part], send_b.at[min(c, 1)], recv_b.at[core, c],
                      place(1, level, spot ^ j))

    def to_level(k, c):
        return remote(last.at[k, c], got_c.at[level], send_c.at[k], recv_c.at[0], place(k, c, spot))

    def received(ref, recv):
        remote(ref, ref, send_f.at[0], recv, partner).wait_recv()

    def sent(ref, send):
        remote(ref, ref, send, recv_f.at[0], partner).wait_send()

    def guarded(condition, action):
        pl.when(condition)(action)

    def send_first():
        for k in range(2):
            gather(first.at[k], 0, k, 0, 0)
            guarded(jnp.logical_not(reducer), lambda k=k: to_first(k).start())

    def send_pair(c):
        gather_level(terms.at[c], 1 - core, c)
        to_partner(c).start()

    def send_plane(c):
        gather_level(mine.at[c], core, c)
        with jax.named_scope("partner_wait"):
            to_partner(c).wait_recv()

        def part_sum(j):
            part = pl.ds(j * share, share)
            mine[c, part, :] = mine[c, part, :] + got_a[c, part, :]
            if j:
                to_plane(c, j).start()
            else:
                guarded(core == 0, lambda: to_plane(c, 0).start())

        for j in list(range(1, plane)) + [0]:
            if c:
                part_sum(j)
            else:
                guarded(spot != j, lambda j=j: part_sum(j))

    def sum_first():
        for k in range(2):
            with jax.named_scope("first_wait"):
                received(got_first.at[k, pl.ds(1, 2 * plane - 1)], recv_f.at[k])
            total = first[k]
            for i in range(1, 2 * plane):
                total = total + got_first[k, i]
            head[k] = total
            if k:
                guarded(level != 0, lambda: to_head(1).start())
            else:
                to_head(0).start()

    def send_level(c):
        with jax.named_scope("plane_wait"):
            received(got_b.at[1, c, pl.ds(share, (plane - 1) * share)], recv_b.at[1, c])
        rows = mine[c, pl.ds(0, share), :]
        for j in range(1, plane):
            rows = rows + got_b[1, c, pl.ds(j * share, share), :]
        last[1, c] = rows
        guarded(level != c, lambda: to_level(1, c).start())
        with jax.named_scope("plane_wait_other"):
            received(got_b.at[0, c], recv_b.at[0, c])
        rows = got_b[0, c, pl.ds(0, share), :]
        for j in range(1, plane):
            rows = rows + got_b[0, c, pl.ds(j * share, share), :]
        last[0, c] = rows
        to_level(0, c).start()

    with jax.named_scope("first_rows"):
        send_first()
    lead = min(3, depth)
    for c in range(lead):
        with jax.named_scope("gather_partner"):
            send_pair(c)
    for c in levels:
        with jax.named_scope("gather_own"):
            send_plane(c)
        if c + lead < depth:
            send_pair(c + lead)

    guarded(reducer, sum_first)
    guarded((core == 1) & (spot != 0), lambda: send_level(0))

    @pl.when(core == 1)
    def _():
        for c in levels[1:]:
            send_level(c)

    is_first = (spot == 0) & (level == 0)
    others = pl.ds(1, depth - 1)

    @pl.when(is_first & (core == 0))
    def _():
        with jax.named_scope("head_wait"):
            received(got_head, recv_h.at[0])
        result = got_head[0]
        for other in range(1, depth):
            result = result + got_head[other]
        out_ref[...] = result

    @pl.when(is_first & (core == 1))
    def _():
        with jax.named_scope("head_wait"):
            received(got_head.at[others], recv_h.at[0])
        result = head[1]
        for other in range(1, depth):
            result = result + got_head[other]
        out_ref[...] = result

    @pl.when(jnp.logical_not(is_first) & (core == 0))
    def _():
        with jax.named_scope("level_wait"):
            received(got_c, recv_c.at[0])
        result = got_c[0]
        for other in range(1, depth):
            result = result + got_c[other]
        out_ref[...] = result

    @pl.when(jnp.logical_not(is_first) & (core == 1))
    def _():
        with jax.named_scope("level_wait"):
            received(got_c.at[others], recv_c.at[0])
        result = last[1, level]
        for r in range(1, depth):
            result = result + got_c[level ^ r]
        out_ref[...] = result

    guarded(jnp.logical_not(reducer), lambda: sent(first, send_f.at[0]))
    guarded(reducer & (level != 0), lambda: sent(head, send_h.at[0]))
    guarded(reducer & (level == 0), lambda: to_head(0).wait_send())
    sent(terms, send_a.at[0])

    @pl.when(core == 0)
    def _():
        sent(mine.at[others], send_b.at[1])
        sent(mine.at[0, pl.ds(0, (plane - 1) * share)], send_b.at[0])

    @pl.when(core == 1)
    def _():
        sent(mine.at[others, pl.ds(share, (plane - 1) * share)], send_b.at[1])
        guarded(spot == 0, lambda: sent(mine.at[0, pl.ds(0, (plane - 1) * share)], send_b.at[0]))
        guarded(spot != 0, lambda: sent(mine.at[0, pl.ds(0, (plane - 2) * share)], send_b.at[0]))
        guarded(spot == 0, lambda: sent(last.at[0, others], send_c.at[0]))
        guarded(spot != 0, lambda: sent(last.at[0], send_c.at[0]))
        fewer = (spot == 0) & (level != 0)
        guarded(fewer, lambda: sent(last.at[1, pl.ds(0, depth - 2)], send_c.at[1]))
        guarded(jnp.logical_not(fewer), lambda: sent(last.at[1, others], send_c.at[1]))


def body(panel, row_signs, sample_rows):
    count, width = panel.shape
    hi_count, lo_count = lax.axis_size("hi"), lax.axis_size("lo")
    kept = sample_rows.shape[0]
    share = kept // (hi_count * lo_count)
    side = 2 ** ((lo_count.bit_length() - 1) // 2)
    depth = lo_count // side
    plane = (hi_count // 2) * side
    loads = len(CUTS) - 1
    vmem = pl.BlockSpec(memory_space=pltpu.VMEM)
    dma = pltpu.SemaphoreType.DMA
    f32 = jnp.float32
    chunk = (depth, plane * share, width)
    return pl.pallas_call(
        functools.partial(kernel, hi_count, lo_count),
        out_shape=pltpu.VMEM((share, width), f32),
        in_specs=[pl.BlockSpec(memory_space=pltpu.HBM)] * 4,
        out_specs=vmem,
        scratch_shapes=[
            pltpu.VMEM((count, width), f32),
            pltpu.VMEM((count // LANES, LANES), f32),
            pltpu.SMEM((kept,), jnp.int32),
            pltpu.VMEM((kept // LANES, LANES), jnp.int32),
            pltpu.VMEM((count, width), f32),
            pltpu.VMEM((LANES, 2 * LANES), jnp.bfloat16),
            pltpu.VMEM((count, width), f32),
            pltpu.VMEM((kept, width), f32),
            pltpu.VMEM(chunk, f32),
            pltpu.VMEM(chunk, f32),
            pltpu.VMEM(chunk, f32),
            pltpu.VMEM((2,) + chunk, f32),
            pltpu.VMEM((depth, share, width), f32),
            pltpu.VMEM((2, depth, share, width), f32),
            pltpu.VMEM((2, share, width), f32),
            pltpu.VMEM((2, 2 * plane, share, width), f32),
            pltpu.VMEM((2, share, width), f32),
            pltpu.VMEM((depth, share, width), f32),
            dma((loads,)), dma((3,)),
            dma((1,)), dma((depth,)),
            dma((2,)), dma((2, depth)),
            dma((2,)), dma((1,)),
            dma((1,)), dma((2,)),
            dma((1,)), dma((1,)),
        ],
        compiler_params=pltpu.CompilerParams(
            collective_id=0, has_side_effects=True, vmem_limit_bytes=60 * 2**20),
        cost_estimate=pl.CostEstimate(
            flops=2 * count * LOW * 2 * width, bytes_accessed=count * width * 4, transcendentals=0),
    )(panel, row_signs.reshape(count // LANES, LANES), sample_rows,
      sample_rows.reshape(kept // LANES, LANES))


def solution(mesh):
    placed = (P(("hi", "lo"), None), P(("hi", "lo"), None), P())
    return jax.shard_map(
        body, mesh=mesh, in_specs=placed, out_specs=P(("hi", "lo"), None), check_vma=False
    )
```

```python
import functools
import math

import jax
import jax.numpy as jnp
from jax import lax
from jax.experimental import pallas as pl
from jax.experimental.pallas import tpu as pltpu
from jax.sharding import PartitionSpec as P

MESH = pl.DeviceIdType.MESH
LOW = 256
LANES = 128
TILE = 8
FUSED = 8
CUTS = (0, 2, 5, 8)


def parity_sign(bits):
    shift = 16
    while shift:
        bits = bits ^ (bits >> shift)
        shift //= 2
    return (1 - 2 * (bits & 1)).astype(jnp.float32)


def kernel(hi_count, lo_count, panel_hbm, signs_hbm, rows_hbm, picks_hbm, out_ref,
           panel, signs_ref, rows_ref, picks_ref, field, had, wide, sgn, terms, mine, got_a, got_b, got_c, last,
           first, got_first, head, got_head, got_far,
           load_sem, small_sem, send_a, recv_a, send_b, recv_b, send_c, recv_c,
           send_f, recv_f, send_h, recv_h, recv_d):
    count = panel.shape[0]
    share = out_ref.shape[0]
    kept = rows_ref.shape[0]
    total = count * hi_count * lo_count
    side = 2 ** ((lo_count.bit_length() - 1) // 2)
    depth = lo_count // side
    plane = (hi_count // 2) * side
    hi, lo = lax.axis_index("hi"), lax.axis_index("lo")
    me = hi * lo_count + lo
    core = hi % 2
    spot = (hi // 2) * side + lo % side
    level = lo // side

    def place(core_to, level_to, spot_to):
        return ((spot_to // side) * 2 + core_to, level_to * side + spot_to % side)

    partner = place(1 - core, level, spot)
    peers_plane = [place(core, level, spot ^ j) for j in range(plane)]
    peers_depth = [place(core, level ^ r, spot) for r in range(depth)]

    loads = load_sem.shape[0]
    groups = count // LANES
    cuts = [c * groups // CUTS[-1] for c in CUTS]
    small = [pltpu.make_async_copy(signs_hbm, signs_ref, small_sem.at[0]),
             pltpu.make_async_copy(picks_hbm, picks_ref, small_sem.at[1]),
             pltpu.make_async_copy(rows_hbm, rows_ref, small_sem.at[2])]
    for copy in small:
        copy.start()

    def load(i):
        part = pl.ds(cuts[i] * LANES, (cuts[i + 1] - cuts[i]) * LANES)
        return pltpu.make_async_copy(panel_hbm.at[part], panel.at[part], load_sem.at[i])

    load(0).start()

    barrier = pltpu.get_barrier_semaphore()
    is_first = (spot == 0) & (level == 0)
    near = depth - 1
    far = (spot == plane - 1) & (level >= near)
    far_devices = [place(k, c, plane - 1) for c in range(near, depth) for k in range(2)]
    cross_plane = [place(1 - core, level, spot ^ j) for j in range(1, plane)]
    cross_depth = [place(1 - core, level ^ r, spot) for r in range(1, depth)]

    def greet(devices):
        for device in devices:
            pl.semaphore_signal(barrier, inc=1, device_id=device, device_id_type=MESH)

    greet([partner])
    pl.when(core == 0)(lambda: greet(cross_depth))
    pl.when(core == 1)(lambda: greet(peers_plane[1:] + cross_plane + peers_depth[1:]))
    pl.when(is_first & (core == 0))(lambda: greet(far_devices))

    left = lax.broadcasted_iota(jnp.int32, (LANES, 2 * LANES), 0)
    right = lax.broadcasted_iota(jnp.int32, (LANES, 2 * LANES), 1)
    had[...] = parity_sign(left & right & (LANES - 1)).astype(jnp.bfloat16)

    for i in range(1, loads):
        load(i).start()

    with jax.named_scope("small_waits"):
        for copy in small:
            copy.wait()

    ahead = 20
    more = 16

    def turn(line):
        return jnp.broadcast_to(line, (LANES, LANES)).T

    def factor(a):
        return turn(signs_ref[pl.ds(a, 1), :])

    with jax.named_scope("early_factors"):
        for a in range(ahead):
            wide[pl.ds(a * LANES, LANES), :] = factor(a)

    ready = ahead
    for i in range(loads):
        with jax.named_scope("load_wait"):
            load(i).wait()
        with jax.named_scope("products"):
            stop = cuts[i + 1]
            later = stop + more + (4 if not i else 0) if i + 1 < loads else stop
            held = []
            lines = []
            if i == loads - 1:
                weight = parity_sign((picks_ref[...] // count) & me) * (1.0 / math.sqrt(total))
                lines = list(range(kept // LANES))
            extra = list(range(max(ready, stop), later))
            for pair in range(cuts[i] // 2, stop // 2):
                big, rest = [], []
                for q in range(2):
                    a = 2 * pair + q
                    rows = pl.ds(a * LANES, LANES)
                    by = wide[rows, :] if a < ready else factor(a)
                    block = panel[rows, :] * by
                    big.append(block.astype(jnp.bfloat16))
                    rest.append((block - big[q].astype(jnp.float32)).astype(jnp.bfloat16))
                both = jnp.concatenate(
                    [jnp.concatenate(big, axis=1), jnp.concatenate(rest, axis=1)], axis=0)
                done = jnp.dot(had[...], both, preferred_element_type=jnp.float32)
                x, y = done[:, :LANES], done[:, LANES:]
                two = [x + y, x - y]
                held.append(two)
                while len(held) > 1 and len(held[-1]) == len(held[-2]):
                    y, x = held.pop(), held.pop()
                    held.append([u + v for u, v in zip(x, y)] + [u - v for u, v in zip(x, y)])
                if len(held[0]) == FUSED:
                    for k, v in enumerate(held.pop()):
                        field[pl.ds((2 * pair + 2 - FUSED + k) * LANES, LANES), :] = v
                if lines:
                    g = lines.pop(0)
                    sgn[pl.ds(g * LANES, LANES), :] = turn(weight[g:g + 1, :])
                if extra and pair % 2 == 0:
                    for a in [extra.pop(0) for _ in range(min(2, len(extra)))]:
                        wide[pl.ds(a * LANES, LANES), :] = factor(a)
            for g in lines:
                sgn[pl.ds(g * LANES, LANES), :] = turn(weight[g:g + 1, :])
            for a in extra:
                wide[pl.ds(a * LANES, LANES), :] = factor(a)
            ready = later

    with jax.named_scope("butterflies"):
        steps = groups // FUSED
        tiles = FUSED * LANES // TILE
        lines = 8

        @pl.loop(0, lines)
        def _(g):
            for t in range(tiles // lines):
                p = g * (tiles // lines) + t
                rows = [pl.ds(b * FUSED * LANES + p * TILE, TILE) for b in range(steps)]
                parts = [field[r, :] for r in rows]
                half = 1
                while half < steps:
                    for b in range(steps):
                        if not b & half:
                            x, y = parts[b], parts[b + half]
                            parts[b], parts[b + half] = x + y, x - y
                    half *= 2
                for b in range(steps):
                    panel[rows[b], :] = parts[b]

    with jax.named_scope("entry_wait"):
        for core_is, expected in ((0, plane), (1, plane + 2 * (depth - 1))):
            pl.when((core == core_is) & far)(lambda n=expected: pl.semaphore_wait(barrier, n + 1))
            pl.when((core == core_is) & jnp.logical_not(far))(lambda n=expected: pl.semaphore_wait(barrier, n))

    def gather(dst, base, core_to, level_to, spot_to):
        hi_to, lo_to = place(core_to, level_to, spot_to)
        start = (hi_to * lo_count + lo_to) * share
        for s in range(share):
            row = rows_ref[start + s] & (count - 1)
            dst[pl.ds(base + s, 1), :] = panel[pl.ds(row, 1), :]
        part = pl.ds(base, share)
        dst[part, :] = dst[part, :] * sgn[pl.ds(start, share), :]

    def gather_level(dst, core_to, level_to):
        @pl.loop(0, plane)
        def _(j):
            if level_to:
                gather(dst, j * share, core_to, level_to, spot ^ j)
            else:
                @pl.when(spot != j)
                def _():
                    gather(dst, j * share, core_to, level_to, spot ^ j)

    def remote(src, dst, send, recv, device):
        return pltpu.make_async_remote_copy(
            src_ref=src, dst_ref=dst, send_sem=send, recv_sem=recv,
            device_id=device, device_id_type=MESH)

    levels = range(depth)

    reducer = (core == 1) & (spot == 0)
    slot = (spot * 2 + core) ^ 1

    def to_first(k):
        return remote(first.at[k], got_first.at[k, slot], send_f.at[0], recv_f.at[k], place(1, level, 0))

    def to_first_chip(k):
        return remote(first.at[k], got_far.at[(level - near) * 2 + core], send_f.at[0], recv_d.at[0], place(k, 0, 0))

    def to_head(k):
        return remote(head.at[k], got_head.at[level], send_h.at[0], recv_h.at[0], place(k, 0, 0))

    def to_partner(c):
        return remote(terms.at[c], got_a.at[c], send_a.at[0], recv_a.at[c], partner)

    def to_plane(c, j):
        part = pl.ds(j * share, share)
        return remote(mine.at[c, part], got_b.at[core, c, part], send_b.at[min(c, 1)], recv_b.at[core, c],
                      place(1, level, spot ^ j))

    def to_level(k, c):
        return remote(last.at[k, c], got_c.at[level], send_c.at[k], recv_c.at[0], place(k, c, spot))

    def received(ref, recv):
        remote(ref, ref, send_f.at[0], recv, partner).wait_recv()

    def sent(ref, send):
        remote(ref, ref, send, recv_f.at[0], partner).wait_send()

    def guarded(condition, action):
        pl.when(condition)(action)

    def send_first():
        for k in range(2):
            gather(first.at[k], 0, k, 0, 0)
            if k:
                guarded(jnp.logical_not(reducer), lambda: to_first(1).start())
            else:
                guarded(jnp.logical_not(reducer | far), lambda: to_first(0).start())
                guarded(far, lambda: to_first_chip(0).start())

    def send_pair(c):
        gather_level(terms.at[c], 1 - core, c)
        to_partner(c).start()

    def send_plane(c):
        gather_level(mine.at[c], core, c)
        with jax.named_scope("partner_wait"):
            to_partner(c).wait_recv()

        def part_sum(j):
            part = pl.ds(j * share, share)
            mine[c, part, :] = mine[c, part, :] + got_a[c, part, :]
            if j:
                to_plane(c, j).start()
            else:
                guarded(core == 0, lambda: to_plane(c, 0).start())

        for j in list(range(1, plane)) + [0]:
            if c:
                part_sum(j)
            else:
                guarded(spot != j, lambda j=j: part_sum(j))

    def sum_first():
        for k in range(2):
            def take(last_slot, k=k):
                with jax.named_scope("first_wait"):
                    received(got_first.at[k, pl.ds(1, last_slot - 1)], recv_f.at[k])
                total = first[k]
                for i in range(1, last_slot):
                    total = total + got_first[k, i]
                head[k] = total

            if k:
                take(2 * plane)
            else:
                guarded(level < near, lambda: take(2 * plane))
                guarded(level >= near, lambda: take(2 * plane - 2))
            if k:
                guarded(level != 0, lambda: to_head(1).start())
            else:
                to_head(0).start()

    def send_level(c):
        with jax.named_scope("plane_wait"):
            received(got_b.at[1, c, pl.ds(share, (plane - 1) * share)], recv_b.at[1, c])
        rows = mine[c, pl.ds(0, share), :]
        for j in range(1, plane):
            rows = rows + got_b[1, c, pl.ds(j * share, share), :]
        last[1, c] = rows
        guarded(level != c, lambda: to_level(1, c).start())
        with jax.named_scope("plane_wait_other"):
            received(got_b.at[0, c], recv_b.at[0, c])
        rows = got_b[0, c, pl.ds(0, share), :]
        for j in range(1, plane):
            rows = rows + got_b[0, c, pl.ds(j * share, share), :]
        last[0, c] = rows
        to_level(0, c).start()

    with jax.named_scope("first_rows"):
        send_first()
    lead = min(3, depth)
    for c in range(lead):
        with jax.named_scope("gather_partner"):
            send_pair(c)
    for c in levels:
        with jax.named_scope("gather_own"):
            send_plane(c)
        if c + lead < depth:
            send_pair(c + lead)

    guarded(reducer, sum_first)
    guarded((core == 1) & (spot != 0), lambda: send_level(0))

    @pl.when(core == 1)
    def _():
        for c in levels[1:]:
            send_level(c)

    others = pl.ds(1, depth - 1)

    @pl.when(is_first & (core == 0))
    def _():
        with jax.named_scope("head_wait"):
            received(got_head, recv_h.at[0])
            received(got_far, recv_d.at[0])
        result = got_head[0]
        for other in range(1, depth):
            result = result + got_head[other]
        for i in range(len(far_devices)):
            result = result + got_far[i]
        out_ref[...] = result

    @pl.when(is_first & (core == 1))
    def _():
        with jax.named_scope("head_wait"):
            received(got_head.at[others], recv_h.at[0])
        result = head[1]
        for other in range(1, depth):
            result = result + got_head[other]
        out_ref[...] = result

    @pl.when(jnp.logical_not(is_first) & (core == 0))
    def _():
        with jax.named_scope("level_wait"):
            received(got_c, recv_c.at[0])
        result = got_c[0]
        for other in range(1, depth):
            result = result + got_c[other]
        out_ref[...] = result

    @pl.when(jnp.logical_not(is_first) & (core == 1))
    def _():
        with jax.named_scope("level_wait"):
            received(got_c.at[others], recv_c.at[0])
        result = last[1, level]
        for r in range(1, depth):
            result = result + got_c[level ^ r]
        out_ref[...] = result

    guarded(jnp.logical_not(reducer), lambda: sent(first, send_f.at[0]))
    guarded(reducer & (level != 0), lambda: sent(head, send_h.at[0]))
    guarded(reducer & (level == 0), lambda: to_head(0).wait_send())
    sent(terms, send_a.at[0])

    @pl.when(core == 0)
    def _():
        sent(mine.at[others], send_b.at[1])
        sent(mine.at[0, pl.ds(0, (plane - 1) * share)], send_b.at[0])

    @pl.when(core == 1)
    def _():
        sent(mine.at[others, pl.ds(share, (plane - 1) * share)], send_b.at[1])
        guarded(spot == 0, lambda: sent(mine.at[0, pl.ds(0, (plane - 1) * share)], send_b.at[0]))
        guarded(spot != 0, lambda: sent(mine.at[0, pl.ds(0, (plane - 2) * share)], send_b.at[0]))
        guarded(spot == 0, lambda: sent(last.at[0, others], send_c.at[0]))
        guarded(spot != 0, lambda: sent(last.at[0], send_c.at[0]))
        fewer = (spot == 0) & (level != 0)
        guarded(fewer, lambda: sent(last.at[1, pl.ds(0, depth - 2)], send_c.at[1]))
        guarded(jnp.logical_not(fewer), lambda: sent(last.at[1, others], send_c.at[1]))


def body(panel, row_signs, sample_rows):
    count, width = panel.shape
    hi_count, lo_count = lax.axis_size("hi"), lax.axis_size("lo")
    kept = sample_rows.shape[0]
    share = kept // (hi_count * lo_count)
    side = 2 ** ((lo_count.bit_length() - 1) // 2)
    depth = lo_count // side
    plane = (hi_count // 2) * side
    loads = len(CUTS) - 1
    vmem = pl.BlockSpec(memory_space=pltpu.VMEM)
    dma = pltpu.SemaphoreType.DMA
    f32 = jnp.float32
    chunk = (depth, plane * share, width)
    return pl.pallas_call(
        functools.partial(kernel, hi_count, lo_count),
        out_shape=pltpu.VMEM((share, width), f32),
        in_specs=[pl.BlockSpec(memory_space=pltpu.HBM)] * 4,
        out_specs=vmem,
        scratch_shapes=[
            pltpu.VMEM((count, width), f32),
            pltpu.VMEM((count // LANES, LANES), f32),
            pltpu.SMEM((kept,), jnp.int32),
            pltpu.VMEM((kept // LANES, LANES), jnp.int32),
            pltpu.VMEM((count, width), f32),
            pltpu.VMEM((LANES, 2 * LANES), jnp.bfloat16),
            pltpu.VMEM((count, width), f32),
            pltpu.VMEM((kept, width), f32),
            pltpu.VMEM(chunk, f32),
            pltpu.VMEM(chunk, f32),
            pltpu.VMEM(chunk, f32),
            pltpu.VMEM((2,) + chunk, f32),
            pltpu.VMEM((depth, share, width), f32),
            pltpu.VMEM((2, depth, share, width), f32),
            pltpu.VMEM((2, share, width), f32),
            pltpu.VMEM((2, 2 * plane, share, width), f32),
            pltpu.VMEM((2, share, width), f32),
            pltpu.VMEM((depth, share, width), f32),
            pltpu.VMEM((2, share, width), f32),
            dma((loads,)), dma((3,)),
            dma((1,)), dma((depth,)),
            dma((2,)), dma((2, depth)),
            dma((2,)), dma((1,)),
            dma((1,)), dma((2,)),
            dma((1,)), dma((1,)),
            dma((1,)),
        ],
        compiler_params=pltpu.CompilerParams(
            collective_id=0, has_side_effects=True, vmem_limit_bytes=60 * 2**20),
        cost_estimate=pl.CostEstimate(
            flops=2 * count * LOW * 2 * width, bytes_accessed=count * width * 4, transcendentals=0),
    )(panel, row_signs.reshape(count // LANES, LANES), sample_rows,
      sample_rows.reshape(kept // LANES, LANES))


def solution(mesh):
    placed = (P(("hi", "lo"), None), P(("hi", "lo"), None), P())
    return jax.shard_map(
        body, mesh=mesh, in_specs=placed, out_specs=P(("hi", "lo"), None), check_vma=False
    )
```

```python
import functools
import math

import jax
import jax.numpy as jnp
from jax import lax
from jax.experimental import pallas as pl
from jax.experimental.pallas import tpu as pltpu
from jax.sharding import PartitionSpec as P

MESH = pl.DeviceIdType.MESH
LOW = 256
LANES = 128
TILE = 8
FUSED = 8
CUTS = (0, 2, 5, 8)


def parity_sign(bits):
    shift = 16
    while shift:
        bits = bits ^ (bits >> shift)
        shift //= 2
    return (1 - 2 * (bits & 1)).astype(jnp.float32)


def kernel(hi_count, lo_count, panel_hbm, signs_hbm, rows_hbm, picks_hbm, out_ref,
           panel, signs_ref, rows_ref, picks_ref, field, had, wide, sgn, terms, mine, got_a, got_b, got_c, last,
           first, got_first, head, got_head, got_far,
           load_sem, small_sem, send_a, recv_a, send_b, recv_b, send_c, recv_c,
           send_f, recv_f, send_h, recv_h, recv_d, entered):
    count = panel.shape[0]
    share = out_ref.shape[0]
    kept = rows_ref.shape[0]
    total = count * hi_count * lo_count
    side = 2 ** ((lo_count.bit_length() - 1) // 2)
    depth = lo_count // side
    plane = (hi_count // 2) * side
    hi, lo = lax.axis_index("hi"), lax.axis_index("lo")
    me = hi * lo_count + lo
    core = hi % 2
    spot = (hi // 2) * side + lo % side
    level = lo // side

    def place(core_to, level_to, spot_to):
        return ((spot_to // side) * 2 + core_to, level_to * side + spot_to % side)

    partner = place(1 - core, level, spot)
    peers_plane = [place(core, level, spot ^ j) for j in range(plane)]
    peers_depth = [place(core, level ^ r, spot) for r in range(depth)]

    loads = load_sem.shape[0]
    groups = count // LANES
    cuts = [c * groups // CUTS[-1] for c in CUTS]
    small = [pltpu.make_async_copy(signs_hbm, signs_ref, small_sem.at[0]),
             pltpu.make_async_copy(picks_hbm, picks_ref, small_sem.at[1]),
             pltpu.make_async_copy(rows_hbm, rows_ref, small_sem.at[2])]
    for copy in small:
        copy.start()

    def load(i):
        part = pl.ds(cuts[i] * LANES, (cuts[i + 1] - cuts[i]) * LANES)
        return pltpu.make_async_copy(panel_hbm.at[part], panel.at[part], load_sem.at[i])

    load(0).start()

    barrier = pltpu.get_barrier_semaphore()
    is_first = (spot == 0) & (level == 0)
    near = depth - 1
    far = (spot == plane - 1) & (level >= near)
    far_devices = [place(k, c, plane - 1) for c in range(near, depth) for k in range(2)]
    cross_plane = [place(1 - core, level, spot ^ j) for j in range(1, plane)]
    cross_depth = [place(1 - core, level ^ r, spot) for r in range(depth)]

    def greet(devices, semaphore=barrier):
        for device in devices:
            pl.semaphore_signal(semaphore, inc=1, device_id=device, device_id_type=MESH)

    def greet_depth(devices, wanted, semaphore=barrier):
        for r in range(1, depth):
            pl.when(wanted(level ^ r))(lambda r=r: greet([peers[r] for peers in devices], semaphore))

    greet([partner])

    @pl.when(core == 0)
    def _():
        greet_depth([cross_depth], lambda other: other > level)

    @pl.when(core == 1)
    def _():
        greet(peers_plane[1:] + cross_plane)
        greet_depth([peers_depth, cross_depth], lambda other: other > level)

    pl.when(is_first & (core == 0))(lambda: greet(far_devices))

    left = lax.broadcasted_iota(jnp.int32, (LANES, 2 * LANES), 0)
    right = lax.broadcasted_iota(jnp.int32, (LANES, 2 * LANES), 1)
    had[...] = parity_sign(left & right & (LANES - 1)).astype(jnp.bfloat16)

    for i in range(1, loads):
        load(i).start()

    with jax.named_scope("small_waits"):
        for copy in small:
            copy.wait()

    ahead = 20
    more = 16

    def turn(line):
        return jnp.broadcast_to(line, (LANES, LANES)).T

    def factor(a):
        return turn(signs_ref[pl.ds(a, 1), :])

    with jax.named_scope("early_factors"):
        for a in range(ahead):
            wide[pl.ds(a * LANES, LANES), :] = factor(a)

    ready = ahead
    for i in range(loads):
        with jax.named_scope("load_wait"):
            load(i).wait()
        with jax.named_scope("products"):
            stop = cuts[i + 1]
            later = stop + more + (4 if not i else 0) if i + 1 < loads else stop
            held = []
            lines = []
            if i == loads - 1:
                weight = parity_sign((picks_ref[...] // count) & me) * (1.0 / math.sqrt(total))
                lines = list(range(kept // LANES))
            extra = list(range(max(ready, stop), later))
            for pair in range(cuts[i] // 2, stop // 2):
                big, rest = [], []
                for q in range(2):
                    a = 2 * pair + q
                    rows = pl.ds(a * LANES, LANES)
                    by = wide[rows, :] if a < ready else factor(a)
                    block = panel[rows, :] * by
                    big.append(block.astype(jnp.bfloat16))
                    rest.append((block - big[q].astype(jnp.float32)).astype(jnp.bfloat16))
                both = jnp.concatenate(
                    [jnp.concatenate(big, axis=1), jnp.concatenate(rest, axis=1)], axis=0)
                done = jnp.dot(had[...], both, preferred_element_type=jnp.float32)
                x, y = done[:, :LANES], done[:, LANES:]
                two = [x + y, x - y]
                held.append(two)
                while len(held) > 1 and len(held[-1]) == len(held[-2]):
                    y, x = held.pop(), held.pop()
                    held.append([u + v for u, v in zip(x, y)] + [u - v for u, v in zip(x, y)])
                if len(held[0]) == FUSED:
                    for k, v in enumerate(held.pop()):
                        field[pl.ds((2 * pair + 2 - FUSED + k) * LANES, LANES), :] = v
                if lines:
                    g = lines.pop(0)
                    sgn[pl.ds(g * LANES, LANES), :] = turn(weight[g:g + 1, :])
                if extra and pair % 2 == 0:
                    for a in [extra.pop(0) for _ in range(min(2, len(extra)))]:
                        wide[pl.ds(a * LANES, LANES), :] = factor(a)
            for g in lines:
                sgn[pl.ds(g * LANES, LANES), :] = turn(weight[g:g + 1, :])
            for a in extra:
                wide[pl.ds(a * LANES, LANES), :] = factor(a)
            ready = later

    with jax.named_scope("butterflies"):
        steps = groups // FUSED
        tiles = FUSED * LANES // TILE
        lines = 8

        @pl.loop(0, lines)
        def _(g):
            for t in range(tiles // lines):
                p = g * (tiles // lines) + t
                rows = [pl.ds(b * FUSED * LANES + p * TILE, TILE) for b in range(steps)]
                parts = [field[r, :] for r in rows]
                half = 1
                while half < steps:
                    for b in range(steps):
                        if not b & half:
                            x, y = parts[b], parts[b + half]
                            parts[b], parts[b + half] = x + y, x - y
                    half *= 2
                for b in range(steps):
                    panel[rows[b], :] = parts[b]

    with jax.named_scope("entry_wait"):
        for core_is, expected in ((0, plane + level), (1, plane + 2 * level)):
            pl.when((core == core_is) & far)(lambda n=expected: pl.semaphore_wait(barrier, n + 1))
            pl.when((core == core_is) & jnp.logical_not(far))(lambda n=expected: pl.semaphore_wait(barrier, n))

    @pl.when(core == 0)
    def _():
        greet_depth([cross_depth], lambda other: other < level, entered.at[0])

    @pl.when(core == 1)
    def _():
        greet_depth([peers_depth], lambda other: other < level, entered.at[0])

    def gather(dst, base, core_to, level_to, spot_to):
        hi_to, lo_to = place(core_to, level_to, spot_to)
        start = (hi_to * lo_count + lo_to) * share
        for s in range(share):
            row = rows_ref[start + s] & (count - 1)
            dst[pl.ds(base + s, 1), :] = panel[pl.ds(row, 1), :]
        part = pl.ds(base, share)
        dst[part, :] = dst[part, :] * sgn[pl.ds(start, share), :]

    def gather_level(dst, core_to, level_to):
        @pl.loop(0, plane)
        def _(j):
            if level_to:
                gather(dst, j * share, core_to, level_to, spot ^ j)
            else:
                @pl.when(spot != j)
                def _():
                    gather(dst, j * share, core_to, level_to, spot ^ j)

    def remote(src, dst, send, recv, device):
        return pltpu.make_async_remote_copy(
            src_ref=src, dst_ref=dst, send_sem=send, recv_sem=recv,
            device_id=device, device_id_type=MESH)

    levels = range(depth)

    reducer = (core == 1) & (spot == 0)
    slot = (spot * 2 + core) ^ 1

    def to_first(k):
        return remote(first.at[k], got_first.at[k, slot], send_f.at[0], recv_f.at[k], place(1, level, 0))

    def to_first_chip(k):
        return remote(first.at[k], got_far.at[(level - near) * 2 + core], send_f.at[0], recv_d.at[0], place(k, 0, 0))

    def to_head(k):
        return remote(head.at[k], got_head.at[level], send_h.at[0], recv_h.at[0], place(k, 0, 0))

    def to_partner(c):
        return remote(terms.at[c], got_a.at[c], send_a.at[0], recv_a.at[c], partner)

    def to_plane(c, j):
        part = pl.ds(j * share, share)
        return remote(mine.at[c, part], got_b.at[core, c, part], send_b.at[min(c, 1)], recv_b.at[core, c],
                      place(1, level, spot ^ j))

    def to_level(k, c):
        return remote(last.at[k, c], got_c.at[level], send_c.at[k], recv_c.at[0], place(k, c, spot))

    def received(ref, recv):
        remote(ref, ref, send_f.at[0], recv, partner).wait_recv()

    def sent(ref, send):
        remote(ref, ref, send, recv_f.at[0], partner).wait_send()

    def guarded(condition, action):
        pl.when(condition)(action)

    def send_first():
        for k in range(2):
            gather(first.at[k], 0, k, 0, 0)
            if k:
                guarded(jnp.logical_not(reducer), lambda: to_first(1).start())
            else:
                guarded(jnp.logical_not(reducer | far), lambda: to_first(0).start())
                guarded(far, lambda: to_first_chip(0).start())

    def send_pair(c):
        gather_level(terms.at[c], 1 - core, c)
        to_partner(c).start()

    def send_plane(c):
        gather_level(mine.at[c], core, c)
        with jax.named_scope("partner_wait"):
            to_partner(c).wait_recv()

        def part_sum(j):
            part = pl.ds(j * share, share)
            mine[c, part, :] = mine[c, part, :] + got_a[c, part, :]
            if j:
                to_plane(c, j).start()
            else:
                guarded(core == 0, lambda: to_plane(c, 0).start())

        for j in list(range(plane - 1, -1, -1)):
            if c:
                part_sum(j)
            else:
                guarded(spot != j, lambda j=j: part_sum(j))

    def sum_first():
        for k in range(2):
            def take(last_slot, k=k):
                with jax.named_scope("first_wait"):
                    received(got_first.at[k, pl.ds(1, last_slot - 1)], recv_f.at[k])
                total = first[k]
                for i in range(1, last_slot):
                    total = total + got_first[k, i]
                head[k] = total

            if k:
                take(2 * plane)
            else:
                guarded(level < near, lambda: take(2 * plane))
                guarded(level >= near, lambda: take(2 * plane - 2))
            if k:
                guarded(level != 0, lambda: to_head(1).start())
            else:
                to_head(0).start()

    def send_level(c):
        with jax.named_scope("plane_wait"):
            received(got_b.at[1, c, pl.ds(share, (plane - 1) * share)], recv_b.at[1, c])
        rows = mine[c, pl.ds(0, share), :]
        for j in range(1, plane):
            rows = rows + got_b[1, c, pl.ds(j * share, share), :]
        last[1, c] = rows
        guarded(level != c, lambda: to_level(1, c).start())
        with jax.named_scope("plane_wait_other"):
            received(got_b.at[0, c], recv_b.at[0, c])
        rows = got_b[0, c, pl.ds(0, share), :]
        for j in range(1, plane):
            rows = rows + got_b[0, c, pl.ds(j * share, share), :]
        last[0, c] = rows
        to_level(0, c).start()

    with jax.named_scope("first_rows"):
        send_first()
    lead = min(3, depth)
    for c in range(lead):
        with jax.named_scope("gather_partner"):
            send_pair(c)
    for c in levels:
        with jax.named_scope("gather_own"):
            send_plane(c)
        if c + lead < depth:
            send_pair(c + lead)

    guarded(reducer, sum_first)
    above = 2 * (depth - 1 - level)
    guarded((core == 1) & (above > 0), lambda: pl.semaphore_wait(entered.at[0], above))
    guarded((core == 1) & (spot != 0), lambda: send_level(0))

    @pl.when(core == 1)
    def _():
        for c in levels[1:]:
            send_level(c)

    others = pl.ds(1, depth - 1)

    @pl.when(is_first & (core == 0))
    def _():
        with jax.named_scope("head_wait"):
            received(got_head, recv_h.at[0])
            received(got_far, recv_d.at[0])
        result = got_head[0]
        for other in range(1, depth):
            result = result + got_head[other]
        for i in range(len(far_devices)):
            result = result + got_far[i]
        out_ref[...] = result

    @pl.when(is_first & (core == 1))
    def _():
        with jax.named_scope("head_wait"):
            received(got_head.at[others], recv_h.at[0])
        result = head[1]
        for other in range(1, depth):
            result = result + got_head[other]
        out_ref[...] = result

    @pl.when(jnp.logical_not(is_first) & (core == 0))
    def _():
        with jax.named_scope("level_wait"):
            received(got_c, recv_c.at[0])
        result = got_c[0]
        for other in range(1, depth):
            result = result + got_c[other]
        out_ref[...] = result

    @pl.when(jnp.logical_not(is_first) & (core == 1))
    def _():
        with jax.named_scope("level_wait"):
            received(got_c.at[others], recv_c.at[0])
        result = last[1, level]
        for r in range(1, depth):
            result = result + got_c[level ^ r]
        out_ref[...] = result

    guarded(jnp.logical_not(reducer), lambda: sent(first, send_f.at[0]))
    guarded(reducer & (level != 0), lambda: sent(head, send_h.at[0]))
    guarded(reducer & (level == 0), lambda: to_head(0).wait_send())
    sent(terms, send_a.at[0])

    @pl.when(core == 0)
    def _():
        sent(mine.at[others], send_b.at[1])
        sent(mine.at[0, pl.ds(0, (plane - 1) * share)], send_b.at[0])

    @pl.when(core == 1)
    def _():
        sent(mine.at[others, pl.ds(share, (plane - 1) * share)], send_b.at[1])
        guarded(spot == 0, lambda: sent(mine.at[0, pl.ds(0, (plane - 1) * share)], send_b.at[0]))
        guarded(spot != 0, lambda: sent(mine.at[0, pl.ds(0, (plane - 2) * share)], send_b.at[0]))
        guarded(spot == 0, lambda: sent(last.at[0, others], send_c.at[0]))
        guarded(spot != 0, lambda: sent(last.at[0], send_c.at[0]))
        fewer = (spot == 0) & (level != 0)
        guarded(fewer, lambda: sent(last.at[1, pl.ds(0, depth - 2)], send_c.at[1]))
        guarded(jnp.logical_not(fewer), lambda: sent(last.at[1, others], send_c.at[1]))


def body(panel, row_signs, sample_rows):
    count, width = panel.shape
    hi_count, lo_count = lax.axis_size("hi"), lax.axis_size("lo")
    kept = sample_rows.shape[0]
    share = kept // (hi_count * lo_count)
    side = 2 ** ((lo_count.bit_length() - 1) // 2)
    depth = lo_count // side
    plane = (hi_count // 2) * side
    loads = len(CUTS) - 1
    vmem = pl.BlockSpec(memory_space=pltpu.VMEM)
    dma = pltpu.SemaphoreType.DMA
    f32 = jnp.float32
    chunk = (depth, plane * share, width)
    return pl.pallas_call(
        functools.partial(kernel, hi_count, lo_count),
        out_shape=pltpu.VMEM((share, width), f32),
        in_specs=[pl.BlockSpec(memory_space=pltpu.HBM)] * 4,
        out_specs=vmem,
        scratch_shapes=[
            pltpu.VMEM((count, width), f32),
            pltpu.VMEM((count // LANES, LANES), f32),
            pltpu.SMEM((kept,), jnp.int32),
            pltpu.VMEM((kept // LANES, LANES), jnp.int32),
            pltpu.VMEM((count, width), f32),
            pltpu.VMEM((LANES, 2 * LANES), jnp.bfloat16),
            pltpu.VMEM((count, width), f32),
            pltpu.VMEM((kept, width), f32),
            pltpu.VMEM(chunk, f32),
            pltpu.VMEM(chunk, f32),
            pltpu.VMEM(chunk, f32),
            pltpu.VMEM((2,) + chunk, f32),
            pltpu.VMEM((depth, share, width), f32),
            pltpu.VMEM((2, depth, share, width), f32),
            pltpu.VMEM((2, share, width), f32),
            pltpu.VMEM((2, 2 * plane, share, width), f32),
            pltpu.VMEM((2, share, width), f32),
            pltpu.VMEM((depth, share, width), f32),
            pltpu.VMEM((2, share, width), f32),
            dma((loads,)), dma((3,)),
            dma((1,)), dma((depth,)),
            dma((2,)), dma((2, depth)),
            dma((2,)), dma((1,)),
            dma((1,)), dma((2,)),
            dma((1,)), dma((1,)),
            dma((1,)), pltpu.SemaphoreType.REGULAR((1,)),
        ],
        compiler_params=pltpu.CompilerParams(
            collective_id=0, has_side_effects=True, vmem_limit_bytes=60 * 2**20),
        cost_estimate=pl.CostEstimate(
            flops=2 * count * LOW * 2 * width, bytes_accessed=count * width * 4, transcendentals=0),
    )(panel, row_signs.reshape(count // LANES, LANES), sample_rows,
      sample_rows.reshape(kept // LANES, LANES))


def solution(mesh):
    placed = (P(("hi", "lo"), None), P(("hi", "lo"), None), P())
    return jax.shard_map(
        body, mesh=mesh, in_specs=placed, out_specs=P(("hi", "lo"), None), check_vma=False
    )
```

```python
import functools
import math

import jax
import jax.numpy as jnp
from jax import lax
from jax.experimental import pallas as pl
from jax.experimental.pallas import tpu as pltpu
from jax.sharding import PartitionSpec as P

MESH = pl.DeviceIdType.MESH
LOW = 256
LANES = 128
TILE = 8
FUSED = 8
CUTS = (0, 2, 5, 8)


def parity_sign(bits):
    shift = 16
    while shift:
        bits = bits ^ (bits >> shift)
        shift //= 2
    return (1 - 2 * (bits & 1)).astype(jnp.float32)


def kernel(hi_count, lo_count, panel_hbm, signs_hbm, rows_hbm, picks_hbm, out_ref,
           panel, signs_ref, rows_ref, picks_ref, field, had, wide, sgn, terms, mine, got_a, got_b, got_c, last,
           first, got_first, head, got_head, got_far,
           load_sem, small_sem, send, recv_a, recv_b, recv_c,
           recv_f, recv_h, recv_d, entered):
    count = panel.shape[0]
    share = out_ref.shape[0]
    kept = rows_ref.shape[0]
    total = count * hi_count * lo_count
    side = 2 ** ((lo_count.bit_length() - 1) // 2)
    depth = lo_count // side
    plane = (hi_count // 2) * side
    hi, lo = lax.axis_index("hi"), lax.axis_index("lo")
    me = hi * lo_count + lo
    core = hi % 2
    spot = (hi // 2) * side + lo % side
    level = lo // side

    def place(core_to, level_to, spot_to):
        return ((spot_to // side) * 2 + core_to, level_to * side + spot_to % side)

    partner = place(1 - core, level, spot)
    peers_plane = [place(core, level, spot ^ j) for j in range(plane)]
    peers_depth = [place(core, level ^ r, spot) for r in range(depth)]

    loads = load_sem.shape[0]
    groups = count // LANES
    cuts = [c * groups // CUTS[-1] for c in CUTS]
    small = [pltpu.make_async_copy(signs_hbm, signs_ref, small_sem.at[0]),
             pltpu.make_async_copy(picks_hbm, picks_ref, small_sem.at[1]),
             pltpu.make_async_copy(rows_hbm, rows_ref, small_sem.at[2])]
    for copy in small:
        copy.start()

    def load(i):
        part = pl.ds(cuts[i] * LANES, (cuts[i + 1] - cuts[i]) * LANES)
        return pltpu.make_async_copy(panel_hbm.at[part], panel.at[part], load_sem.at[i])

    load(0).start()

    barrier = pltpu.get_barrier_semaphore()
    is_first = (spot == 0) & (level == 0)
    near = depth - 1
    far = (spot == plane - 1) & (level >= near)
    far_devices = [place(k, c, plane - 1) for c in range(near, depth) for k in range(2)]
    cross_plane = [place(1 - core, level, spot ^ j) for j in range(1, plane)]
    cross_depth = [place(1 - core, level ^ r, spot) for r in range(depth)]

    def greet(devices, semaphore=barrier):
        for device in devices:
            pl.semaphore_signal(semaphore, inc=1, device_id=device, device_id_type=MESH)

    def greet_depth(devices, wanted, semaphore=barrier):
        for r in range(1, depth):
            pl.when(wanted(level ^ r))(lambda r=r: greet([peers[r] for peers in devices], semaphore))

    greet([partner])

    @pl.when(core == 0)
    def _():
        greet_depth([cross_depth], lambda other: other > level)

    @pl.when(core == 1)
    def _():
        greet(peers_plane[1:] + cross_plane)
        greet_depth([peers_depth, cross_depth], lambda other: other > level)

    pl.when(is_first & (core == 0))(lambda: greet(far_devices))

    left = lax.broadcasted_iota(jnp.int32, (LANES, 2 * LANES), 0)
    right = lax.broadcasted_iota(jnp.int32, (LANES, 2 * LANES), 1)
    had[...] = parity_sign(left & right & (LANES - 1)).astype(jnp.bfloat16)

    for i in range(1, loads):
        load(i).start()

    with jax.named_scope("small_waits"):
        for copy in small:
            copy.wait()

    ahead = 20
    more = 16

    def turn(line):
        return jnp.broadcast_to(line, (LANES, LANES)).T

    def factor(a):
        return turn(signs_ref[pl.ds(a, 1), :])

    with jax.named_scope("early_factors"):
        for a in range(ahead):
            wide[pl.ds(a * LANES, LANES), :] = factor(a)

    ready = ahead
    for i in range(loads):
        with jax.named_scope("load_wait"):
            load(i).wait()
        with jax.named_scope("products"):
            stop = cuts[i + 1]
            later = stop + more + (4 if not i else 0) if i + 1 < loads else stop
            held = []
            lines = []
            if i == loads - 1:
                weight = parity_sign((picks_ref[...] // count) & me) * (1.0 / math.sqrt(total))
                lines = list(range(kept // LANES))
            extra = list(range(max(ready, stop), later))
            for pair in range(cuts[i] // 2, stop // 2):
                big, rest = [], []
                for q in range(2):
                    a = 2 * pair + q
                    rows = pl.ds(a * LANES, LANES)
                    by = wide[rows, :] if a < ready else factor(a)
                    block = panel[rows, :] * by
                    big.append(block.astype(jnp.bfloat16))
                    rest.append((block - big[q].astype(jnp.float32)).astype(jnp.bfloat16))
                both = jnp.concatenate(
                    [jnp.concatenate(big, axis=1), jnp.concatenate(rest, axis=1)], axis=0)
                done = jnp.dot(had[...], both, preferred_element_type=jnp.float32)
                x, y = done[:, :LANES], done[:, LANES:]
                two = [x + y, x - y]
                held.append(two)
                while len(held) > 1 and len(held[-1]) == len(held[-2]):
                    y, x = held.pop(), held.pop()
                    held.append([u + v for u, v in zip(x, y)] + [u - v for u, v in zip(x, y)])
                if len(held[0]) == FUSED:
                    for k, v in enumerate(held.pop()):
                        field[pl.ds((2 * pair + 2 - FUSED + k) * LANES, LANES), :] = v
                if lines:
                    g = lines.pop(0)
                    sgn[pl.ds(g * LANES, LANES), :] = turn(weight[g:g + 1, :])
                if extra and pair % 2 == 0:
                    for a in [extra.pop(0) for _ in range(min(2, len(extra)))]:
                        wide[pl.ds(a * LANES, LANES), :] = factor(a)
            for g in lines:
                sgn[pl.ds(g * LANES, LANES), :] = turn(weight[g:g + 1, :])
            for a in extra:
                wide[pl.ds(a * LANES, LANES), :] = factor(a)
            ready = later

    with jax.named_scope("butterflies"):
        steps = groups // FUSED
        tiles = FUSED * LANES // TILE
        lines = 8

        @pl.loop(0, lines)
        def _(g):
            for t in range(tiles // lines):
                p = g * (tiles // lines) + t
                rows = [pl.ds(b * FUSED * LANES + p * TILE, TILE) for b in range(steps)]
                parts = [field[r, :] for r in rows]
                half = 1
                while half < steps:
                    for b in range(steps):
                        if not b & half:
                            x, y = parts[b], parts[b + half]
                            parts[b], parts[b + half] = x + y, x - y
                    half *= 2
                for b in range(steps):
                    panel[rows[b], :] = parts[b]

    with jax.named_scope("entry_wait"):
        for core_is, expected in ((0, plane + level), (1, plane + 2 * level)):
            pl.when((core == core_is) & far)(lambda n=expected: pl.semaphore_wait(barrier, n + 1))
            pl.when((core == core_is) & jnp.logical_not(far))(lambda n=expected: pl.semaphore_wait(barrier, n))

    @pl.when(core == 0)
    def _():
        greet_depth([cross_depth], lambda other: other < level, entered.at[0])

    @pl.when(core == 1)
    def _():
        greet_depth([peers_depth], lambda other: other < level, entered.at[0])

    def gather(dst, base, core_to, level_to, spot_to):
        hi_to, lo_to = place(core_to, level_to, spot_to)
        start = (hi_to * lo_count + lo_to) * share
        for s in range(share):
            row = rows_ref[start + s] & (count - 1)
            dst[pl.ds(base + s, 1), :] = panel[pl.ds(row, 1), :]
        part = pl.ds(base, share)
        dst[part, :] = dst[part, :] * sgn[pl.ds(start, share), :]

    def gather_level(dst, core_to, level_to):
        @pl.loop(0, plane)
        def _(j):
            if level_to:
                gather(dst, j * share, core_to, level_to, spot ^ j)
            else:
                @pl.when(spot != j)
                def _():
                    gather(dst, j * share, core_to, level_to, spot ^ j)

    def remote(src, dst, done, recv, device):
        return pltpu.make_async_remote_copy(
            src_ref=src, dst_ref=dst, send_sem=done, recv_sem=recv,
            device_id=device, device_id_type=MESH)

    levels = range(depth)

    reducer = (core == 1) & (spot == 0)
    slot = (spot * 2 + core) ^ 1

    def to_first(k):
        return remote(first.at[k], got_first.at[k, slot], send.at[0], recv_f.at[k], place(1, level, 0))

    def to_first_chip(k):
        return remote(first.at[k], got_far.at[(level - near) * 2 + core], send.at[0], recv_d.at[0], place(k, 0, 0))

    def to_head(k):
        return remote(head.at[k], got_head.at[level], send.at[0], recv_h.at[0], place(k, 0, 0))

    def to_partner(c):
        return remote(terms.at[c], got_a.at[c], send.at[0], recv_a.at[c], partner)

    def to_plane(c, j):
        part = pl.ds(j * share, share)
        return remote(mine.at[c, part], got_b.at[core, c, part], send.at[0], recv_b.at[core, c],
                      place(1, level, spot ^ j))

    def to_level(k, c):
        return remote(last.at[k, c], got_c.at[level], send.at[0], recv_c.at[0], place(k, c, spot))

    def received(ref, recv):
        remote(ref, ref, send.at[0], recv, partner).wait_recv()

    def guarded(condition, action):
        pl.when(condition)(action)

    def send_first():
        for k in range(2):
            gather(first.at[k], 0, k, 0, 0)
            if k:
                guarded(jnp.logical_not(reducer), lambda: to_first(1).start())
            else:
                guarded(jnp.logical_not(reducer | far), lambda: to_first(0).start())
                guarded(far, lambda: to_first_chip(0).start())

    def send_pair(c):
        gather_level(terms.at[c], 1 - core, c)
        to_partner(c).start()

    def send_plane(c):
        gather_level(mine.at[c], core, c)
        with jax.named_scope("partner_wait"):
            to_partner(c).wait_recv()

        def part_sum(j):
            part = pl.ds(j * share, share)
            mine[c, part, :] = mine[c, part, :] + got_a[c, part, :]
            if j:
                to_plane(c, j).start()
            else:
                guarded(core == 0, lambda: to_plane(c, 0).start())

        for j in list(range(plane - 1, -1, -1)):
            if c:
                part_sum(j)
            else:
                guarded(spot != j, lambda j=j: part_sum(j))

    def sum_first():
        for k in range(2):
            def take(last_slot, k=k):
                with jax.named_scope("first_wait"):
                    received(got_first.at[k, pl.ds(1, last_slot - 1)], recv_f.at[k])
                total = first[k]
                for i in range(1, last_slot):
                    total = total + got_first[k, i]
                head[k] = total

            if k:
                take(2 * plane)
            else:
                guarded(level < near, lambda: take(2 * plane))
                guarded(level >= near, lambda: take(2 * plane - 2))
            if k:
                guarded(level != 0, lambda: to_head(1).start())
            else:
                to_head(0).start()

    def send_level(c):
        with jax.named_scope("plane_wait"):
            received(got_b.at[1, c, pl.ds(share, (plane - 1) * share)], recv_b.at[1, c])
        rows = mine[c, pl.ds(0, share), :]
        for j in range(1, plane):
            rows = rows + got_b[1, c, pl.ds(j * share, share), :]
        last[1, c] = rows
        guarded(level != c, lambda: to_level(1, c).start())
        with jax.named_scope("plane_wait_other"):
            received(got_b.at[0, c], recv_b.at[0, c])
        rows = got_b[0, c, pl.ds(0, share), :]
        for j in range(1, plane):
            rows = rows + got_b[0, c, pl.ds(j * share, share), :]
        last[0, c] = rows
        to_level(0, c).start()

    with jax.named_scope("first_rows"):
        send_first()
    lead = min(3, depth)
    for c in range(lead):
        with jax.named_scope("gather_partner"):
            send_pair(c)
    for c in levels:
        with jax.named_scope("gather_own"):
            send_plane(c)
        if c + lead < depth:
            send_pair(c + lead)

    guarded(reducer, sum_first)
    above = 2 * (depth - 1 - level)
    guarded((core == 1) & (above > 0), lambda: pl.semaphore_wait(entered.at[0], above))
    guarded((core == 1) & (spot != 0), lambda: send_level(0))

    @pl.when(core == 1)
    def _():
        for c in levels[1:]:
            send_level(c)

    others = pl.ds(1, depth - 1)

    @pl.when(is_first & (core == 0))
    def _():
        with jax.named_scope("head_wait"):
            received(got_head, recv_h.at[0])
            received(got_far, recv_d.at[0])
        result = got_head[0]
        for other in range(1, depth):
            result = result + got_head[other]
        for i in range(len(far_devices)):
            result = result + got_far[i]
        out_ref[...] = result

    @pl.when(is_first & (core == 1))
    def _():
        with jax.named_scope("head_wait"):
            received(got_head.at[others], recv_h.at[0])
        result = head[1]
        for other in range(1, depth):
            result = result + got_head[other]
        out_ref[...] = result

    @pl.when(jnp.logical_not(is_first) & (core == 0))
    def _():
        with jax.named_scope("level_wait"):
            received(got_c, recv_c.at[0])
        result = got_c[0]
        for other in range(1, depth):
            result = result + got_c[other]
        out_ref[...] = result

    @pl.when(jnp.logical_not(is_first) & (core == 1))
    def _():
        with jax.named_scope("level_wait"):
            received(got_c.at[others], recv_c.at[0])
        result = last[1, level]
        for r in range(1, depth):
            result = result + got_c[level ^ r]
        out_ref[...] = result

    def all_sent(blocks):
        ref = panel.at[pl.ds(0, blocks * share)]
        remote(ref, ref, send.at[0], recv_d.at[0], partner).wait_send()

    pairs = plane * depth
    onward = plane + 2 * (depth - 1)
    pl.when(core == 0)(lambda: all_sent(2 * pairs + 1))
    guarded((core == 1) & (spot == 0), lambda: all_sent(2 * pairs - plane - depth + 1 + onward))
    guarded((core == 1) & (spot != 0), lambda: all_sent(2 * pairs - plane - depth + 1 + onward + 1))


def body(panel, row_signs, sample_rows):
    count, width = panel.shape
    hi_count, lo_count = lax.axis_size("hi"), lax.axis_size("lo")
    kept = sample_rows.shape[0]
    share = kept // (hi_count * lo_count)
    side = 2 ** ((lo_count.bit_length() - 1) // 2)
    depth = lo_count // side
    plane = (hi_count // 2) * side
    loads = len(CUTS) - 1
    vmem = pl.BlockSpec(memory_space=pltpu.VMEM)
    dma = pltpu.SemaphoreType.DMA
    f32 = jnp.float32
    chunk = (depth, plane * share, width)
    return pl.pallas_call(
        functools.partial(kernel, hi_count, lo_count),
        out_shape=pltpu.VMEM((share, width), f32),
        in_specs=[pl.BlockSpec(memory_space=pltpu.HBM)] * 4,
        out_specs=vmem,
        scratch_shapes=[
            pltpu.VMEM((count, width), f32),
            pltpu.VMEM((count // LANES, LANES), f32),
            pltpu.SMEM((kept,), jnp.int32),
            pltpu.VMEM((kept // LANES, LANES), jnp.int32),
            pltpu.VMEM((count, width), f32),
            pltpu.VMEM((LANES, 2 * LANES), jnp.bfloat16),
            pltpu.VMEM((count, width), f32),
            pltpu.VMEM((kept, width), f32),
            pltpu.VMEM(chunk, f32),
            pltpu.VMEM(chunk, f32),
            pltpu.VMEM(chunk, f32),
            pltpu.VMEM((2,) + chunk, f32),
            pltpu.VMEM((depth, share, width), f32),
            pltpu.VMEM((2, depth, share, width), f32),
            pltpu.VMEM((2, share, width), f32),
            pltpu.VMEM((2, 2 * plane, share, width), f32),
            pltpu.VMEM((2, share, width), f32),
            pltpu.VMEM((depth, share, width), f32),
            pltpu.VMEM((2, share, width), f32),
            dma((loads,)), dma((3,)),
            dma((1,)), dma((depth,)), dma((2, depth)), dma((1,)),
            dma((2,)), dma((1,)), dma((1,)), pltpu.SemaphoreType.REGULAR((1,)),
        ],
        compiler_params=pltpu.CompilerParams(
            collective_id=0, has_side_effects=True, vmem_limit_bytes=60 * 2**20),
        cost_estimate=pl.CostEstimate(
            flops=2 * count * LOW * 2 * width, bytes_accessed=count * width * 4, transcendentals=0),
    )(panel, row_signs.reshape(count // LANES, LANES), sample_rows,
      sample_rows.reshape(kept // LANES, LANES))


def solution(mesh):
    placed = (P(("hi", "lo"), None), P(("hi", "lo"), None), P())
    return jax.shard_map(
        body, mesh=mesh, in_specs=placed, out_specs=P(("hi", "lo"), None), check_vma=False
    )
```

```python
import functools
import math

import jax
import jax.numpy as jnp
from jax import lax
from jax.experimental import pallas as pl
from jax.experimental.pallas import tpu as pltpu
from jax.sharding import PartitionSpec as P

MESH = pl.DeviceIdType.MESH
LOW = 256
LANES = 128
TILE = 8
FUSED = 8
CUTS = (0, 2, 5, 8)


def parity_sign(bits):
    shift = 16
    while shift:
        bits = bits ^ (bits >> shift)
        shift //= 2
    return (1 - 2 * (bits & 1)).astype(jnp.float32)


def kernel(hi_count, lo_count, panel_hbm, signs_hbm, rows_hbm, picks_hbm, out_ref,
           panel, signs_ref, rows_ref, picks_ref, field, had, wide, sgn, terms, mine, got_a, got_b, got_c, last,
           first, got_first, head, got_head, got_far,
           load_sem, small_sem, send, recv_a, recv_b, recv_c,
           recv_f, recv_h, recv_d, entered):
    count = panel.shape[0]
    share = out_ref.shape[0]
    kept = rows_ref.shape[0]
    total = count * hi_count * lo_count
    side = 2 ** ((lo_count.bit_length() - 1) // 2)
    depth = lo_count // side
    plane = (hi_count // 2) * side
    hi, lo = lax.axis_index("hi"), lax.axis_index("lo")
    me = hi * lo_count + lo
    core = hi % 2
    spot = (hi // 2) * side + lo % side
    level = lo // side

    def place(core_to, level_to, spot_to):
        return ((spot_to // side) * 2 + core_to, level_to * side + spot_to % side)

    partner = place(1 - core, level, spot)
    peers_plane = [place(core, level, spot ^ j) for j in range(plane)]
    peers_depth = [place(core, level ^ r, spot) for r in range(depth)]

    loads = load_sem.shape[0]
    groups = count // LANES
    cuts = [c * groups // CUTS[-1] for c in CUTS]
    small = [pltpu.make_async_copy(signs_hbm, signs_ref, small_sem.at[0]),
             pltpu.make_async_copy(picks_hbm, picks_ref, small_sem.at[1]),
             pltpu.make_async_copy(rows_hbm, rows_ref, small_sem.at[2])]
    for copy in small:
        copy.start()

    def load(i):
        part = pl.ds(cuts[i] * LANES, (cuts[i + 1] - cuts[i]) * LANES)
        return pltpu.make_async_copy(panel_hbm.at[part], panel.at[part], load_sem.at[i])

    load(0).start()

    barrier = pltpu.get_barrier_semaphore()
    is_first = (spot == 0) & (level == 0)
    near = depth - 1
    far = (core == 0) & (spot == plane - 1) & (level >= near)
    far_devices = [place(0, c, plane - 1) for c in range(near, depth)]
    cross_plane = [place(1 - core, level, spot ^ j) for j in range(1, plane)]
    cross_depth = [place(1 - core, level ^ r, spot) for r in range(depth)]

    def greet(devices, semaphore=barrier):
        for device in devices:
            pl.semaphore_signal(semaphore, inc=1, device_id=device, device_id_type=MESH)

    def greet_depth(devices, wanted, semaphore=barrier):
        for r in range(1, depth):
            pl.when(wanted(level ^ r))(lambda r=r: greet([peers[r] for peers in devices], semaphore))

    greet([partner])

    @pl.when(core == 0)
    def _():
        greet_depth([cross_depth], lambda other: other > level)

    @pl.when(core == 1)
    def _():
        greet(peers_plane[1:] + cross_plane)
        greet_depth([peers_depth, cross_depth], lambda other: other > level)

    pl.when(is_first)(lambda: greet(far_devices))

    left = lax.broadcasted_iota(jnp.int32, (LANES, 2 * LANES), 0)
    right = lax.broadcasted_iota(jnp.int32, (LANES, 2 * LANES), 1)
    had[...] = parity_sign(left & right & (LANES - 1)).astype(jnp.bfloat16)

    for i in range(1, loads):
        load(i).start()

    with jax.named_scope("small_waits"):
        for copy in small:
            copy.wait()

    ahead = 20
    more = 16

    def turn(line):
        return jnp.broadcast_to(line, (LANES, LANES)).T

    def factor(a):
        return turn(signs_ref[pl.ds(a, 1), :])

    with jax.named_scope("early_factors"):
        for a in range(ahead):
            wide[pl.ds(a * LANES, LANES), :] = factor(a)

    ready = ahead
    for i in range(loads):
        with jax.named_scope("load_wait"):
            load(i).wait()
        with jax.named_scope("products"):
            stop = cuts[i + 1]
            later = stop + more + (4 if not i else 0) if i + 1 < loads else stop
            held = []
            lines = []
            if i == loads - 1:
                weight = parity_sign((picks_ref[...] // count) & me) * (1.0 / math.sqrt(total))
                lines = list(range(kept // LANES))
            extra = list(range(max(ready, stop), later))
            for pair in range(cuts[i] // 2, stop // 2):
                big, rest = [], []
                for q in range(2):
                    a = 2 * pair + q
                    rows = pl.ds(a * LANES, LANES)
                    by = wide[rows, :] if a < ready else factor(a)
                    block = panel[rows, :] * by
                    big.append(block.astype(jnp.bfloat16))
                    rest.append((block - big[q].astype(jnp.float32)).astype(jnp.bfloat16))
                both = jnp.concatenate(
                    [jnp.concatenate(big, axis=1), jnp.concatenate(rest, axis=1)], axis=0)
                done = jnp.dot(had[...], both, preferred_element_type=jnp.float32)
                x, y = done[:, :LANES], done[:, LANES:]
                two = [x + y, x - y]
                held.append(two)
                while len(held) > 1 and len(held[-1]) == len(held[-2]):
                    y, x = held.pop(), held.pop()
                    held.append([u + v for u, v in zip(x, y)] + [u - v for u, v in zip(x, y)])
                if len(held[0]) == FUSED:
                    for k, v in enumerate(held.pop()):
                        field[pl.ds((2 * pair + 2 - FUSED + k) * LANES, LANES), :] = v
                if lines:
                    g = lines.pop(0)
                    sgn[pl.ds(g * LANES, LANES), :] = turn(weight[g:g + 1, :])
                if extra and pair % 2 == 0:
                    for a in [extra.pop(0) for _ in range(min(2, len(extra)))]:
                        wide[pl.ds(a * LANES, LANES), :] = factor(a)
            for g in lines:
                sgn[pl.ds(g * LANES, LANES), :] = turn(weight[g:g + 1, :])
            for a in extra:
                wide[pl.ds(a * LANES, LANES), :] = factor(a)
            ready = later

    with jax.named_scope("butterflies"):
        steps = groups // FUSED
        tiles = FUSED * LANES // TILE
        lines = 8

        @pl.loop(0, lines)
        def _(g):
            for t in range(tiles // lines):
                p = g * (tiles // lines) + t
                rows = [pl.ds(b * FUSED * LANES + p * TILE, TILE) for b in range(steps)]
                parts = [field[r, :] for r in rows]
                half = 1
                while half < steps:
                    for b in range(steps):
                        if not b & half:
                            x, y = parts[b], parts[b + half]
                            parts[b], parts[b + half] = x + y, x - y
                    half *= 2
                for b in range(steps):
                    panel[rows[b], :] = parts[b]

    with jax.named_scope("entry_wait"):
        for core_is, expected in ((0, plane + level), (1, plane + 2 * level)):
            pl.when((core == core_is) & far)(lambda n=expected: pl.semaphore_wait(barrier, n + 2))
            pl.when((core == core_is) & jnp.logical_not(far))(lambda n=expected: pl.semaphore_wait(barrier, n))

    @pl.when(core == 0)
    def _():
        greet_depth([cross_depth], lambda other: other < level, entered.at[0])

    @pl.when(core == 1)
    def _():
        greet_depth([peers_depth], lambda other: other < level, entered.at[0])

    def gather(dst, base, core_to, level_to, spot_to):
        hi_to, lo_to = place(core_to, level_to, spot_to)
        start = (hi_to * lo_count + lo_to) * share
        for s in range(share):
            row = rows_ref[start + s] & (count - 1)
            dst[pl.ds(base + s, 1), :] = panel[pl.ds(row, 1), :]
        part = pl.ds(base, share)
        dst[part, :] = dst[part, :] * sgn[pl.ds(start, share), :]

    def gather_level(dst, core_to, level_to):
        @pl.loop(0, plane)
        def _(j):
            if level_to:
                gather(dst, j * share, core_to, level_to, spot ^ j)
            else:
                @pl.when(spot != j)
                def _():
                    gather(dst, j * share, core_to, level_to, spot ^ j)

    def remote(src, dst, done, recv, device):
        return pltpu.make_async_remote_copy(
            src_ref=src, dst_ref=dst, send_sem=done, recv_sem=recv,
            device_id=device, device_id_type=MESH)

    levels = range(depth)

    reducer = (core == 1) & (spot == 0)
    slot = (spot * 2 + core) ^ 1

    def to_first(k):
        return remote(first.at[k], got_first.at[k, slot], send.at[0], recv_f.at[k], place(1, level, 0))

    def to_first_chip(k):
        return remote(first.at[k], got_far.at[level - near], send.at[0], recv_d.at[0], place(k, 0, 0))

    def to_head(k):
        return remote(head.at[k], got_head.at[level], send.at[0], recv_h.at[0], place(k, 0, 0))

    def to_partner(c):
        return remote(terms.at[c], got_a.at[c], send.at[0], recv_a.at[c], partner)

    def to_plane(c, j):
        part = pl.ds(j * share, share)
        return remote(mine.at[c, part], got_b.at[core, c, part], send.at[0], recv_b.at[core, c],
                      place(1, level, spot ^ j))

    def to_level(k, c):
        return remote(last.at[k, c], got_c.at[level], send.at[0], recv_c.at[0], place(k, c, spot))

    def received(ref, recv):
        remote(ref, ref, send.at[0], recv, partner).wait_recv()

    def guarded(condition, action):
        pl.when(condition)(action)

    def send_first():
        for k in range(2):
            gather(first.at[k], 0, k, 0, 0)
            guarded(jnp.logical_not(reducer | far), lambda k=k: to_first(k).start())
            guarded(far, lambda k=k: to_first_chip(k).start())

    def send_pair(c):
        gather_level(terms.at[c], 1 - core, c)
        to_partner(c).start()

    def send_plane(c):
        gather_level(mine.at[c], core, c)
        with jax.named_scope("partner_wait"):
            to_partner(c).wait_recv()

        def part_sum(j):
            part = pl.ds(j * share, share)
            mine[c, part, :] = mine[c, part, :] + got_a[c, part, :]
            if j:
                to_plane(c, j).start()
            else:
                guarded(core == 0, lambda: to_plane(c, 0).start())

        for j in list(range(plane - 1, -1, -1)):
            if c:
                part_sum(j)
            else:
                guarded(spot != j, lambda j=j: part_sum(j))

    def sum_first():
        for k in range(2):
            def take(last_slot, k=k):
                with jax.named_scope("first_wait"):
                    received(got_first.at[k, pl.ds(1, last_slot - 1)], recv_f.at[k])
                total = first[k]
                for i in range(1, last_slot):
                    total = total + got_first[k, i]
                head[k] = total

            guarded(level < near, lambda: take(2 * plane))
            guarded(level >= near, lambda: take(2 * plane - 1))
            if k:
                guarded(level != 0, lambda: to_head(1).start())
            else:
                to_head(0).start()

    def send_level(c):
        with jax.named_scope("plane_wait"):
            received(got_b.at[1, c, pl.ds(share, (plane - 1) * share)], recv_b.at[1, c])
        rows = mine[c, pl.ds(0, share), :]
        for j in range(1, plane):
            rows = rows + got_b[1, c, pl.ds(j * share, share), :]
        last[1, c] = rows
        guarded(level != c, lambda: to_level(1, c).start())
        with jax.named_scope("plane_wait_other"):
            received(got_b.at[0, c], recv_b.at[0, c])
        rows = got_b[0, c, pl.ds(0, share), :]
        for j in range(1, plane):
            rows = rows + got_b[0, c, pl.ds(j * share, share), :]
        last[0, c] = rows
        to_level(0, c).start()

    with jax.named_scope("first_rows"):
        send_first()
    lead = min(3, depth)
    for c in range(lead):
        with jax.named_scope("gather_partner"):
            send_pair(c)
    for c in levels:
        with jax.named_scope("gather_own"):
            send_plane(c)
        if c + lead < depth:
            send_pair(c + lead)

    guarded(reducer, sum_first)
    above = 2 * (depth - 1 - level)
    guarded((core == 1) & (above > 0), lambda: pl.semaphore_wait(entered.at[0], above))
    guarded((core == 1) & (spot != 0), lambda: send_level(0))

    @pl.when(core == 1)
    def _():
        for c in levels[1:]:
            send_level(c)

    others = pl.ds(1, depth - 1)

    @pl.when(is_first & (core == 0))
    def _():
        with jax.named_scope("head_wait"):
            received(got_head, recv_h.at[0])
            received(got_far, recv_d.at[0])
        result = got_head[0]
        for other in range(1, depth):
            result = result + got_head[other]
        for i in range(len(far_devices)):
            result = result + got_far[i]
        out_ref[...] = result

    @pl.when(is_first & (core == 1))
    def _():
        with jax.named_scope("head_wait"):
            received(got_head.at[others], recv_h.at[0])
            received(got_far, recv_d.at[0])
        result = head[1]
        for other in range(1, depth):
            result = result + got_head[other]
        for i in range(len(far_devices)):
            result = result + got_far[i]
        out_ref[...] = result

    @pl.when(jnp.logical_not(is_first) & (core == 0))
    def _():
        with jax.named_scope("level_wait"):
            received(got_c, recv_c.at[0])
        result = got_c[0]
        for other in range(1, depth):
            result = result + got_c[other]
        out_ref[...] = result

    @pl.when(jnp.logical_not(is_first) & (core == 1))
    def _():
        with jax.named_scope("level_wait"):
            received(got_c.at[others], recv_c.at[0])
        result = last[1, level]
        for r in range(1, depth):
            result = result + got_c[level ^ r]
        out_ref[...] = result

    def all_sent(blocks):
        ref = panel.at[pl.ds(0, blocks * share)]
        remote(ref, ref, send.at[0], recv_d.at[0], partner).wait_send()

    pairs = plane * depth
    onward = plane + 2 * (depth - 1)
    pl.when(core == 0)(lambda: all_sent(2 * pairs + 1))
    guarded((core == 1) & (spot == 0), lambda: all_sent(2 * pairs - plane - depth + 1 + onward))
    guarded((core == 1) & (spot != 0), lambda: all_sent(2 * pairs - plane - depth + 1 + onward + 1))


def body(panel, row_signs, sample_rows):
    count, width = panel.shape
    hi_count, lo_count = lax.axis_size("hi"), lax.axis_size("lo")
    kept = sample_rows.shape[0]
    share = kept // (hi_count * lo_count)
    side = 2 ** ((lo_count.bit_length() - 1) // 2)
    depth = lo_count // side
    plane = (hi_count // 2) * side
    loads = len(CUTS) - 1
    vmem = pl.BlockSpec(memory_space=pltpu.VMEM)
    dma = pltpu.SemaphoreType.DMA
    f32 = jnp.float32
    chunk = (depth, plane * share, width)
    return pl.pallas_call(
        functools.partial(kernel, hi_count, lo_count),
        out_shape=pltpu.VMEM((share, width), f32),
        in_specs=[pl.BlockSpec(memory_space=pltpu.HBM)] * 4,
        out_specs=vmem,
        scratch_shapes=[
            pltpu.VMEM((count, width), f32),
            pltpu.VMEM((count // LANES, LANES), f32),
            pltpu.SMEM((kept,), jnp.int32),
            pltpu.VMEM((kept // LANES, LANES), jnp.int32),
            pltpu.VMEM((count, width), f32),
            pltpu.VMEM((LANES, 2 * LANES), jnp.bfloat16),
            pltpu.VMEM((count, width), f32),
            pltpu.VMEM((kept, width), f32),
            pltpu.VMEM(chunk, f32),
            pltpu.VMEM(chunk, f32),
            pltpu.VMEM(chunk, f32),
            pltpu.VMEM((2,) + chunk, f32),
            pltpu.VMEM((depth, share, width), f32),
            pltpu.VMEM((2, depth, share, width), f32),
            pltpu.VMEM((2, share, width), f32),
            pltpu.VMEM((2, 2 * plane, share, width), f32),
            pltpu.VMEM((2, share, width), f32),
            pltpu.VMEM((depth, share, width), f32),
            pltpu.VMEM((1, share, width), f32),
            dma((loads,)), dma((3,)),
            dma((1,)), dma((depth,)), dma((2, depth)), dma((1,)),
            dma((2,)), dma((1,)), dma((1,)), pltpu.SemaphoreType.REGULAR((1,)),
        ],
        compiler_params=pltpu.CompilerParams(
            collective_id=0, has_side_effects=True, vmem_limit_bytes=60 * 2**20),
        cost_estimate=pl.CostEstimate(
            flops=2 * count * LOW * 2 * width, bytes_accessed=count * width * 4, transcendentals=0),
    )(panel, row_signs.reshape(count // LANES, LANES), sample_rows,
      sample_rows.reshape(kept // LANES, LANES))


def solution(mesh):
    placed = (P(("hi", "lo"), None), P(("hi", "lo"), None), P())
    return jax.shard_map(
        body, mesh=mesh, in_specs=placed, out_specs=P(("hi", "lo"), None), check_vma=False
    )
```

```python
import functools
import math

import jax
import jax.numpy as jnp
from jax import lax
from jax.experimental import pallas as pl
from jax.experimental.pallas import tpu as pltpu
from jax.sharding import PartitionSpec as P

MESH = pl.DeviceIdType.MESH
LOW = 256
LANES = 128
TILE = 8
FUSED = 8
CUTS = (0, 2, 5, 8)


def parity_sign(bits):
    shift = 16
    while shift:
        bits = bits ^ (bits >> shift)
        shift //= 2
    return (1 - 2 * (bits & 1)).astype(jnp.float32)


def kernel(hi_count, lo_count, panel_hbm, signs_hbm, rows_hbm, picks_hbm, out_ref,
           panel, signs_ref, rows_ref, picks_ref, field, had, wide, sgn, terms, mine, got_a, got_b, got_c, last,
           first, got_first, head, got_head, got_far,
           load_sem, small_sem, send, recv_a, recv_b, recv_c,
           recv_f, recv_h, recv_d, entered):
    count = panel.shape[0]
    share = out_ref.shape[0]
    kept = rows_ref.shape[0]
    total = count * hi_count * lo_count
    side = 2 ** ((lo_count.bit_length() - 1) // 2)
    depth = lo_count // side
    plane = (hi_count // 2) * side
    hi, lo = lax.axis_index("hi"), lax.axis_index("lo")
    me = hi * lo_count + lo
    core = hi % 2
    spot = (hi // 2) * side + lo % side
    level = lo // side

    def place(core_to, level_to, spot_to):
        return ((spot_to // side) * 2 + core_to, level_to * side + spot_to % side)

    partner = place(1 - core, level, spot)
    peers_plane = [place(core, level, spot ^ j) for j in range(plane)]
    peers_depth = [place(core, level ^ r, spot) for r in range(depth)]

    loads = load_sem.shape[0]
    groups = count // LANES
    cuts = [c * groups // CUTS[-1] for c in CUTS]
    small = [pltpu.make_async_copy(signs_hbm, signs_ref, small_sem.at[0]),
             pltpu.make_async_copy(picks_hbm, picks_ref, small_sem.at[1]),
             pltpu.make_async_copy(rows_hbm, rows_ref, small_sem.at[2])]
    for copy in small:
        copy.start()

    def load(i):
        part = pl.ds(cuts[i] * LANES, (cuts[i + 1] - cuts[i]) * LANES)
        return pltpu.make_async_copy(panel_hbm.at[part], panel.at[part], load_sem.at[i])

    load(0).start()

    barrier = pltpu.get_barrier_semaphore()
    is_first = (spot == 0) & (level == 0)
    near = depth - 1
    far = (core == 0) & (spot == plane - 1) & (level >= near)
    far_devices = [place(0, c, plane - 1) for c in range(near, depth)]
    cross_plane = [place(1 - core, level, spot ^ j) for j in range(1, plane)]
    cross_depth = [place(1 - core, level ^ r, spot) for r in range(depth)]

    def greet(devices, semaphore=barrier):
        for device in devices:
            pl.semaphore_signal(semaphore, inc=1, device_id=device, device_id_type=MESH)

    def greet_depth(devices, wanted, semaphore=barrier):
        for r in range(1, depth):
            pl.when(wanted(level ^ r))(lambda r=r: greet([peers[r] for peers in devices], semaphore))

    greet([partner])

    @pl.when(core == 0)
    def _():
        greet_depth([cross_depth], lambda other: other > level)

    @pl.when(core == 1)
    def _():
        greet(peers_plane[1:] + cross_plane)
        greet_depth([peers_depth, cross_depth], lambda other: other > level)

    pl.when(is_first)(lambda: greet(far_devices))

    for i in range(1, loads):
        load(i).start()

    left = lax.broadcasted_iota(jnp.int32, (LANES, 2 * LANES), 0)
    right = lax.broadcasted_iota(jnp.int32, (LANES, 2 * LANES), 1)
    had[...] = parity_sign(left & right & (LANES - 1)).astype(jnp.bfloat16)

    with jax.named_scope("small_waits"):
        for copy in small:
            copy.wait()

    ahead = 20
    more = 16

    def turn(line):
        return jnp.broadcast_to(line, (LANES, LANES)).T

    def factor(a):
        return turn(signs_ref[pl.ds(a, 1), :])

    with jax.named_scope("early_factors"):
        for a in range(ahead):
            wide[pl.ds(a * LANES, LANES), :] = factor(a)

    ready = ahead
    for i in range(loads):
        with jax.named_scope("load_wait"):
            load(i).wait()
        with jax.named_scope("products"):
            stop = cuts[i + 1]
            later = stop + more + (4 if not i else 0) if i + 1 < loads else stop
            held = []
            lines = []
            if i == loads - 1:
                weight = parity_sign((picks_ref[...] // count) & me) * (1.0 / math.sqrt(total))
                lines = list(range(kept // LANES))
            extra = list(range(max(ready, stop), later))
            for pair in range(cuts[i] // 2, stop // 2):
                big, rest = [], []
                for q in range(2):
                    a = 2 * pair + q
                    rows = pl.ds(a * LANES, LANES)
                    by = wide[rows, :] if a < ready else factor(a)
                    block = panel[rows, :] * by
                    big.append(block.astype(jnp.bfloat16))
                    rest.append((block - big[q].astype(jnp.float32)).astype(jnp.bfloat16))
                both = jnp.concatenate(
                    [jnp.concatenate(big, axis=1), jnp.concatenate(rest, axis=1)], axis=0)
                done = jnp.dot(had[...], both, preferred_element_type=jnp.float32)
                x, y = done[:, :LANES], done[:, LANES:]
                two = [x + y, x - y]
                held.append(two)
                while len(held) > 1 and len(held[-1]) == len(held[-2]):
                    y, x = held.pop(), held.pop()
                    held.append([u + v for u, v in zip(x, y)] + [u - v for u, v in zip(x, y)])
                if len(held[0]) == FUSED:
                    for k, v in enumerate(held.pop()):
                        field[pl.ds((2 * pair + 2 - FUSED + k) * LANES, LANES), :] = v
                if lines:
                    g = lines.pop(0)
                    sgn[pl.ds(g * LANES, LANES), :] = turn(weight[g:g + 1, :])
                if extra and pair % 2 == 0:
                    for a in [extra.pop(0) for _ in range(min(2, len(extra)))]:
                        wide[pl.ds(a * LANES, LANES), :] = factor(a)
            for g in lines:
                sgn[pl.ds(g * LANES, LANES), :] = turn(weight[g:g + 1, :])
            for a in extra:
                wide[pl.ds(a * LANES, LANES), :] = factor(a)
            ready = later

    with jax.named_scope("butterflies"):
        steps = groups // FUSED
        tiles = FUSED * LANES // TILE
        lines = 8

        @pl.loop(0, lines)
        def _(g):
            for t in range(tiles // lines):
                p = g * (tiles // lines) + t
                rows = [pl.ds(b * FUSED * LANES + p * TILE, TILE) for b in range(steps)]
                parts = [field[r, :] for r in rows]
                half = 1
                while half < steps:
                    for b in range(steps):
                        if not b & half:
                            x, y = parts[b], parts[b + half]
                            parts[b], parts[b + half] = x + y, x - y
                    half *= 2
                for b in range(steps):
                    panel[rows[b], :] = parts[b]

    with jax.named_scope("entry_wait"):
        for core_is, expected in ((0, plane + level), (1, plane + 2 * level)):
            pl.when((core == core_is) & far)(lambda n=expected: pl.semaphore_wait(barrier, n + 2))
            pl.when((core == core_is) & jnp.logical_not(far))(lambda n=expected: pl.semaphore_wait(barrier, n))

    @pl.when(core == 0)
    def _():
        greet_depth([cross_depth], lambda other: other < level, entered.at[0])

    @pl.when(core == 1)
    def _():
        greet_depth([peers_depth], lambda other: other < level, entered.at[0])

    def gather(dst, base, core_to, level_to, spot_to):
        hi_to, lo_to = place(core_to, level_to, spot_to)
        start = (hi_to * lo_count + lo_to) * share
        for s in range(share):
            row = rows_ref[start + s] & (count - 1)
            dst[pl.ds(base + s, 1), :] = panel[pl.ds(row, 1), :]
        part = pl.ds(base, share)
        dst[part, :] = dst[part, :] * sgn[pl.ds(start, share), :]

    def gather_level(dst, core_to, level_to):
        @pl.loop(0, plane)
        def _(j):
            if level_to:
                gather(dst, j * share, core_to, level_to, spot ^ j)
            else:
                @pl.when(spot != j)
                def _():
                    gather(dst, j * share, core_to, level_to, spot ^ j)

    def remote(src, dst, done, recv, device):
        return pltpu.make_async_remote_copy(
            src_ref=src, dst_ref=dst, send_sem=done, recv_sem=recv,
            device_id=device, device_id_type=MESH)

    levels = range(depth)

    reducer = (core == 1) & (spot == 0)
    slot = (spot * 2 + core) ^ 1

    def to_first(k):
        return remote(first.at[k], got_first.at[k, slot], send.at[0], recv_f.at[k], place(1, level, 0))

    def to_first_chip(k):
        return remote(first.at[k], got_far.at[level - near], send.at[0], recv_d.at[0], place(k, 0, 0))

    def to_head(k):
        return remote(head.at[k], got_head.at[level], send.at[0], recv_h.at[0], place(k, 0, 0))

    def to_partner(c):
        return remote(terms.at[c], got_a.at[c], send.at[0], recv_a.at[c], partner)

    def to_plane(c, j):
        part = pl.ds(j * share, share)
        return remote(mine.at[c, part], got_b.at[core, c, part], send.at[0], recv_b.at[core, c],
                      place(1, level, spot ^ j))

    def to_level(k, c):
        return remote(last.at[k, c], got_c.at[level], send.at[0], recv_c.at[0], place(k, c, spot))

    def received(ref, recv):
        remote(ref, ref, send.at[0], recv, partner).wait_recv()

    def guarded(condition, action):
        pl.when(condition)(action)

    def send_first():
        for k in range(2):
            gather(first.at[k], 0, k, 0, 0)
            guarded(jnp.logical_not(reducer | far), lambda k=k: to_first(k).start())
            guarded(far, lambda k=k: to_first_chip(k).start())

    def send_pair(c):
        gather_level(terms.at[c], 1 - core, c)
        to_partner(c).start()

    def send_plane(c):
        gather_level(mine.at[c], core, c)
        with jax.named_scope("partner_wait"):
            to_partner(c).wait_recv()

        def part_sum(j):
            part = pl.ds(j * share, share)
            mine[c, part, :] = mine[c, part, :] + got_a[c, part, :]
            if j:
                to_plane(c, j).start()
            else:
                guarded(core == 0, lambda: to_plane(c, 0).start())

        for j in list(range(plane - 1, -1, -1)):
            if c:
                part_sum(j)
            else:
                guarded(spot != j, lambda j=j: part_sum(j))

    def sum_first():
        for k in range(2):
            def take(last_slot, k=k):
                with jax.named_scope("first_wait"):
                    received(got_first.at[k, pl.ds(1, last_slot - 1)], recv_f.at[k])
                total = first[k]
                for i in range(1, last_slot):
                    total = total + got_first[k, i]
                head[k] = total

            guarded(level < near, lambda: take(2 * plane))
            guarded(level >= near, lambda: take(2 * plane - 1))
            if k:
                guarded(level != 0, lambda: to_head(1).start())
            else:
                to_head(0).start()

    def send_level(c):
        with jax.named_scope("plane_wait"):
            received(got_b.at[1, c, pl.ds(share, (plane - 1) * share)], recv_b.at[1, c])
        rows = mine[c, pl.ds(0, share), :]
        for j in range(1, plane):
            rows = rows + got_b[1, c, pl.ds(j * share, share), :]
        last[1, c] = rows
        guarded(level != c, lambda: to_level(1, c).start())
        with jax.named_scope("plane_wait_other"):
            received(got_b.at[0, c], recv_b.at[0, c])
        rows = got_b[0, c, pl.ds(0, share), :]
        for j in range(1, plane):
            rows = rows + got_b[0, c, pl.ds(j * share, share), :]
        last[0, c] = rows
        to_level(0, c).start()

    with jax.named_scope("first_rows"):
        send_first()
    lead = min(3, depth)
    for c in range(lead):
        with jax.named_scope("gather_partner"):
            send_pair(c)
    for c in levels:
        with jax.named_scope("gather_own"):
            send_plane(c)
        if c + lead < depth:
            send_pair(c + lead)

    guarded(reducer, sum_first)
    above = 2 * (depth - 1 - level)
    guarded((core == 1) & (above > 0), lambda: pl.semaphore_wait(entered.at[0], above))
    guarded((core == 1) & (spot != 0), lambda: send_level(0))

    @pl.when(core == 1)
    def _():
        for c in levels[1:]:
            send_level(c)

    others = pl.ds(1, depth - 1)

    @pl.when(is_first & (core == 0))
    def _():
        with jax.named_scope("head_wait"):
            received(got_head, recv_h.at[0])
            received(got_far, recv_d.at[0])
        result = got_head[0]
        for other in range(1, depth):
            result = result + got_head[other]
        for i in range(len(far_devices)):
            result = result + got_far[i]
        out_ref[...] = result

    @pl.when(is_first & (core == 1))
    def _():
        with jax.named_scope("head_wait"):
            received(got_head.at[others], recv_h.at[0])
            received(got_far, recv_d.at[0])
        result = head[1]
        for other in range(1, depth):
            result = result + got_head[other]
        for i in range(len(far_devices)):
            result = result + got_far[i]
        out_ref[...] = result

    @pl.when(jnp.logical_not(is_first) & (core == 0))
    def _():
        with jax.named_scope("level_wait"):
            received(got_c, recv_c.at[0])
        result = got_c[0]
        for other in range(1, depth):
            result = result + got_c[other]
        out_ref[...] = result

    @pl.when(jnp.logical_not(is_first) & (core == 1))
    def _():
        with jax.named_scope("level_wait"):
            received(got_c.at[others], recv_c.at[0])
        result = last[1, level]
        for r in range(1, depth):
            result = result + got_c[level ^ r]
        out_ref[...] = result

    def all_sent(blocks):
        ref = panel.at[pl.ds(0, blocks * share)]
        remote(ref, ref, send.at[0], recv_d.at[0], partner).wait_send()

    pairs = plane * depth
    onward = plane + 2 * (depth - 1)
    pl.when(core == 0)(lambda: all_sent(2 * pairs + 1))
    guarded((core == 1) & (spot == 0), lambda: all_sent(2 * pairs - plane - depth + 1 + onward))
    guarded((core == 1) & (spot != 0), lambda: all_sent(2 * pairs - plane - depth + 1 + onward + 1))


def body(panel, row_signs, sample_rows):
    count, width = panel.shape
    hi_count, lo_count = lax.axis_size("hi"), lax.axis_size("lo")
    kept = sample_rows.shape[0]
    share = kept // (hi_count * lo_count)
    side = 2 ** ((lo_count.bit_length() - 1) // 2)
    depth = lo_count // side
    plane = (hi_count // 2) * side
    loads = len(CUTS) - 1
    vmem = pl.BlockSpec(memory_space=pltpu.VMEM)
    dma = pltpu.SemaphoreType.DMA
    f32 = jnp.float32
    chunk = (depth, plane * share, width)
    return pl.pallas_call(
        functools.partial(kernel, hi_count, lo_count),
        out_shape=pltpu.VMEM((share, width), f32),
        in_specs=[pl.BlockSpec(memory_space=pltpu.HBM)] * 4,
        out_specs=vmem,
        scratch_shapes=[
            pltpu.VMEM((count, width), f32),
            pltpu.VMEM((count // LANES, LANES), f32),
            pltpu.SMEM((kept,), jnp.int32),
            pltpu.VMEM((kept // LANES, LANES), jnp.int32),
            pltpu.VMEM((count, width), f32),
            pltpu.VMEM((LANES, 2 * LANES), jnp.bfloat16),
            pltpu.VMEM((count, width), f32),
            pltpu.VMEM((kept, width), f32),
            pltpu.VMEM(chunk, f32),
            pltpu.VMEM(chunk, f32),
            pltpu.VMEM(chunk, f32),
            pltpu.VMEM((2,) + chunk, f32),
            pltpu.VMEM((depth, share, width), f32),
            pltpu.VMEM((2, depth, share, width), f32),
            pltpu.VMEM((2, share, width), f32),
            pltpu.VMEM((2, 2 * plane, share, width), f32),
            pltpu.VMEM((2, share, width), f32),
            pltpu.VMEM((depth, share, width), f32),
            pltpu.VMEM((1, share, width), f32),
            dma((loads,)), dma((3,)),
            dma((1,)), dma((depth,)), dma((2, depth)), dma((1,)),
            dma((2,)), dma((1,)), dma((1,)), pltpu.SemaphoreType.REGULAR((1,)),
        ],
        compiler_params=pltpu.CompilerParams(
            collective_id=0, has_side_effects=True, vmem_limit_bytes=60 * 2**20),
        cost_estimate=pl.CostEstimate(
            flops=2 * count * LOW * 2 * width, bytes_accessed=count * width * 4, transcendentals=0),
    )(panel, row_signs.reshape(count // LANES, LANES), sample_rows,
      sample_rows.reshape(kept // LANES, LANES))


def solution(mesh):
    placed = (P(("hi", "lo"), None), P(("hi", "lo"), None), P())
    return jax.shard_map(
        body, mesh=mesh, in_specs=placed, out_specs=P(("hi", "lo"), None), check_vma=False
    )
```

```python
import functools
import math

import jax
import jax.numpy as jnp
from jax import lax
from jax.experimental import pallas as pl
from jax.experimental.pallas import tpu as pltpu
from jax.sharding import PartitionSpec as P

MESH = pl.DeviceIdType.MESH
LOW = 256
LANES = 128
TILE = 8
FUSED = 8
CUTS = (0, 2, 5, 8)


def parity_sign(bits):
    shift = 16
    while shift:
        bits = bits ^ (bits >> shift)
        shift //= 2
    return (1 - 2 * (bits & 1)).astype(jnp.float32)


def kernel(hi_count, lo_count, panel_hbm, signs_hbm, rows_hbm, picks_hbm, out_ref,
           panel, signs_ref, rows_ref, picks_ref, field, had, wide, sgn, terms, mine, got_a, got_b, got_c, last,
           first, got_first, head, got_head, got_far,
           load_sem, small_sem, send, recv_a, recv_b, recv_c,
           recv_f, recv_h, recv_d, entered):
    count = panel.shape[0]
    share = out_ref.shape[0]
    kept = rows_ref.shape[0]
    total = count * hi_count * lo_count
    side = 2 ** ((lo_count.bit_length() - 1) // 2)
    depth = lo_count // side
    plane = (hi_count // 2) * side
    hi, lo = lax.axis_index("hi"), lax.axis_index("lo")
    me = hi * lo_count + lo
    core = hi % 2
    spot = (hi // 2) * side + lo % side
    level = lo // side

    def place(core_to, level_to, spot_to):
        return ((spot_to // side) * 2 + core_to, level_to * side + spot_to % side)

    partner = place(1 - core, level, spot)
    peers_plane = [place(core, level, spot ^ j) for j in range(plane)]
    peers_depth = [place(core, level ^ r, spot) for r in range(depth)]

    loads = load_sem.shape[0]
    groups = count // LANES
    cuts = [c * groups // CUTS[-1] for c in CUTS]
    small = [pltpu.make_async_copy(signs_hbm, signs_ref, small_sem.at[0]),
             pltpu.make_async_copy(picks_hbm, picks_ref, small_sem.at[1]),
             pltpu.make_async_copy(rows_hbm, rows_ref, small_sem.at[2])]
    for copy in small:
        copy.start()

    def load(i):
        part = pl.ds(cuts[i] * LANES, (cuts[i + 1] - cuts[i]) * LANES)
        return pltpu.make_async_copy(panel_hbm.at[part], panel.at[part], load_sem.at[i])

    load(0).start()

    barrier = pltpu.get_barrier_semaphore()
    is_first = (spot == 0) & (level == 0)
    near = depth - 1
    far = (core == 0) & (spot == plane - 1) & (level >= near)
    far_devices = [place(0, c, plane - 1) for c in range(near, depth)]
    cross_plane = [place(1 - core, level, spot ^ j) for j in range(1, plane)]
    cross_depth = [place(1 - core, level ^ r, spot) for r in range(depth)]

    def greet(devices, semaphore=barrier):
        for device in devices:
            pl.semaphore_signal(semaphore, inc=1, device_id=device, device_id_type=MESH)

    def greet_depth(devices, wanted, semaphore=barrier):
        for r in range(1, depth):
            pl.when(wanted(level ^ r))(lambda r=r: greet([peers[r] for peers in devices], semaphore))

    greet([partner])

    @pl.when(core == 0)
    def _():
        greet_depth([cross_depth], lambda other: other > level)

    @pl.when(core == 1)
    def _():
        greet(peers_plane[1:] + cross_plane)
        greet_depth([peers_depth, cross_depth], lambda other: other > level)

    pl.when(is_first)(lambda: greet(far_devices))

    for i in range(1, loads):
        load(i).start()

    left = lax.broadcasted_iota(jnp.int32, (LANES, 2 * LANES), 0)
    right = lax.broadcasted_iota(jnp.int32, (LANES, 2 * LANES), 1)
    had[...] = parity_sign(left & right & (LANES - 1)).astype(jnp.bfloat16)

    with jax.named_scope("small_waits"):
        for copy in small:
            copy.wait()

    ahead = 20
    more = 16

    def turn(line):
        return jnp.broadcast_to(line, (LANES, LANES)).T

    def factor(a):
        return turn(signs_ref[pl.ds(a, 1), :])

    with jax.named_scope("early_factors"):
        for a in range(ahead):
            wide[pl.ds(a * LANES, LANES), :] = factor(a)

    ready = ahead
    for i in range(loads):
        with jax.named_scope("load_wait"):
            load(i).wait()
        with jax.named_scope("products"):
            stop = cuts[i + 1]
            later = stop + more + (4 if not i else 0) if i + 1 < loads else stop
            held = []
            lines = []
            if i == loads - 1:
                weight = parity_sign((picks_ref[...] // count) & me) * (1.0 / math.sqrt(total))
                lines = list(range(kept // LANES))
            extra = list(range(max(ready, stop), later))
            for pair in range(cuts[i] // 2, stop // 2):
                big, rest = [], []
                for q in range(2):
                    a = 2 * pair + q
                    rows = pl.ds(a * LANES, LANES)
                    by = wide[rows, :] if a < ready else factor(a)
                    block = panel[rows, :] * by
                    big.append(block.astype(jnp.bfloat16))
                    rest.append((block - big[q].astype(jnp.float32)).astype(jnp.bfloat16))
                both = jnp.concatenate(
                    [jnp.concatenate(big, axis=1), jnp.concatenate(rest, axis=1)], axis=0)
                done = jnp.dot(had[...], both, preferred_element_type=jnp.float32)
                x, y = done[:, :LANES], done[:, LANES:]
                two = [x + y, x - y]
                held.append(two)
                while len(held) > 1 and len(held[-1]) == len(held[-2]):
                    y, x = held.pop(), held.pop()
                    held.append([u + v for u, v in zip(x, y)] + [u - v for u, v in zip(x, y)])
                if len(held[0]) == FUSED:
                    for k, v in enumerate(held.pop()):
                        field[pl.ds((2 * pair + 2 - FUSED + k) * LANES, LANES), :] = v
                if lines:
                    g = lines.pop(0)
                    sgn[pl.ds(g * LANES, LANES), :] = turn(weight[g:g + 1, :])
                if extra and pair % 2 == 0:
                    for a in [extra.pop(0) for _ in range(min(2, len(extra)))]:
                        wide[pl.ds(a * LANES, LANES), :] = factor(a)
            for g in lines:
                sgn[pl.ds(g * LANES, LANES), :] = turn(weight[g:g + 1, :])
            for a in extra:
                wide[pl.ds(a * LANES, LANES), :] = factor(a)
            ready = later

    with jax.named_scope("butterflies"):
        steps = groups // FUSED
        tiles = FUSED * LANES // TILE
        lines = 4

        @pl.loop(0, lines)
        def _(g):
            for t in range(tiles // lines):
                p = g * (tiles // lines) + t
                rows = [pl.ds(b * FUSED * LANES + p * TILE, TILE) for b in range(steps)]
                parts = [field[r, :] for r in rows]
                half = 1
                while half < steps:
                    for b in range(steps):
                        if not b & half:
                            x, y = parts[b], parts[b + half]
                            parts[b], parts[b + half] = x + y, x - y
                    half *= 2
                for b in range(steps):
                    panel[rows[b], :] = parts[b]

    with jax.named_scope("entry_wait"):
        for core_is, expected in ((0, plane + level), (1, plane + 2 * level)):
            pl.when((core == core_is) & far)(lambda n=expected: pl.semaphore_wait(barrier, n + 2))
            pl.when((core == core_is) & jnp.logical_not(far))(lambda n=expected: pl.semaphore_wait(barrier, n))

    @pl.when(core == 0)
    def _():
        greet_depth([cross_depth], lambda other: other < level, entered.at[0])

    @pl.when(core == 1)
    def _():
        greet_depth([peers_depth], lambda other: other < level, entered.at[0])

    def gather(dst, base, core_to, level_to, spot_to):
        hi_to, lo_to = place(core_to, level_to, spot_to)
        start = (hi_to * lo_count + lo_to) * share
        for s in range(share):
            row = rows_ref[start + s] & (count - 1)
            dst[pl.ds(base + s, 1), :] = panel[pl.ds(row, 1), :]
        part = pl.ds(base, share)
        dst[part, :] = dst[part, :] * sgn[pl.ds(start, share), :]

    def gather_level(dst, core_to, level_to):
        @pl.loop(0, plane)
        def _(j):
            if level_to:
                gather(dst, j * share, core_to, level_to, spot ^ j)
            else:
                @pl.when(spot != j)
                def _():
                    gather(dst, j * share, core_to, level_to, spot ^ j)

    def remote(src, dst, done, recv, device):
        return pltpu.make_async_remote_copy(
            src_ref=src, dst_ref=dst, send_sem=done, recv_sem=recv,
            device_id=device, device_id_type=MESH)

    levels = range(depth)

    reducer = (core == 1) & (spot == 0)
    slot = (spot * 2 + core) ^ 1

    def to_first(k):
        return remote(first.at[k], got_first.at[k, slot], send.at[0], recv_f.at[k], place(1, level, 0))

    def to_first_chip(k):
        return remote(first.at[k], got_far.at[level - near], send.at[0], recv_d.at[0], place(k, 0, 0))

    def to_head(k):
        return remote(head.at[k], got_head.at[level], send.at[0], recv_h.at[0], place(k, 0, 0))

    def to_partner(c):
        return remote(terms.at[c], got_a.at[c], send.at[0], recv_a.at[c], partner)

    def to_plane(c, j):
        part = pl.ds(j * share, share)
        return remote(mine.at[c, part], got_b.at[core, c, part], send.at[0], recv_b.at[core, c],
                      place(1, level, spot ^ j))

    def to_level(k, c):
        return remote(last.at[k, c], got_c.at[level], send.at[0], recv_c.at[0], place(k, c, spot))

    def received(ref, recv):
        remote(ref, ref, send.at[0], recv, partner).wait_recv()

    def guarded(condition, action):
        pl.when(condition)(action)

    def send_first():
        for k in range(2):
            gather(first.at[k], 0, k, 0, 0)
            guarded(jnp.logical_not(reducer | far), lambda k=k: to_first(k).start())
            guarded(far, lambda k=k: to_first_chip(k).start())

    def send_pair(c):
        gather_level(terms.at[c], 1 - core, c)
        to_partner(c).start()

    def send_plane(c):
        gather_level(mine.at[c], core, c)
        with jax.named_scope("partner_wait"):
            to_partner(c).wait_recv()

        def part_sum(j):
            part = pl.ds(j * share, share)
            mine[c, part, :] = mine[c, part, :] + got_a[c, part, :]
            if j:
                to_plane(c, j).start()
            else:
                guarded(core == 0, lambda: to_plane(c, 0).start())

        for j in list(range(plane - 1, -1, -1)):
            if c:
                part_sum(j)
            else:
                guarded(spot != j, lambda j=j: part_sum(j))

    def sum_first():
        for k in range(2):
            def take(last_slot, k=k):
                with jax.named_scope("first_wait"):
                    received(got_first.at[k, pl.ds(1, last_slot - 1)], recv_f.at[k])
                total = first[k]
                for i in range(1, last_slot):
                    total = total + got_first[k, i]
                head[k] = total

            guarded(level < near, lambda: take(2 * plane))
            guarded(level >= near, lambda: take(2 * plane - 1))
            if k:
                guarded(level != 0, lambda: to_head(1).start())
            else:
                to_head(0).start()

    def send_level(c):
        with jax.named_scope("plane_wait"):
            received(got_b.at[1, c, pl.ds(share, (plane - 1) * share)], recv_b.at[1, c])
        rows = mine[c, pl.ds(0, share), :]
        for j in range(1, plane):
            rows = rows + got_b[1, c, pl.ds(j * share, share), :]
        last[1, c] = rows
        guarded(level != c, lambda: to_level(1, c).start())
        with jax.named_scope("plane_wait_other"):
            received(got_b.at[0, c], recv_b.at[0, c])
        rows = got_b[0, c, pl.ds(0, share), :]
        for j in range(1, plane):
            rows = rows + got_b[0, c, pl.ds(j * share, share), :]
        last[0, c] = rows
        to_level(0, c).start()

    with jax.named_scope("first_rows"):
        send_first()
    lead = min(3, depth)
    for c in range(lead):
        with jax.named_scope("gather_partner"):
            send_pair(c)
    for c in levels:
        with jax.named_scope("gather_own"):
            send_plane(c)
        if c + lead < depth:
            send_pair(c + lead)

    guarded(reducer, sum_first)
    above = 2 * (depth - 1 - level)
    guarded((core == 1) & (above > 0), lambda: pl.semaphore_wait(entered.at[0], above))
    guarded((core == 1) & (spot != 0), lambda: send_level(0))

    @pl.when(core == 1)
    def _():
        for c in levels[1:]:
            send_level(c)

    others = pl.ds(1, depth - 1)

    @pl.when(is_first & (core == 0))
    def _():
        with jax.named_scope("head_wait"):
            received(got_head, recv_h.at[0])
            received(got_far, recv_d.at[0])
        result = got_head[0]
        for other in range(1, depth):
            result = result + got_head[other]
        for i in range(len(far_devices)):
            result = result + got_far[i]
        out_ref[...] = result

    @pl.when(is_first & (core == 1))
    def _():
        with jax.named_scope("head_wait"):
            received(got_head.at[others], recv_h.at[0])
            received(got_far, recv_d.at[0])
        result = head[1]
        for other in range(1, depth):
            result = result + got_head[other]
        for i in range(len(far_devices)):
            result = result + got_far[i]
        out_ref[...] = result

    @pl.when(jnp.logical_not(is_first) & (core == 0))
    def _():
        with jax.named_scope("level_wait"):
            received(got_c, recv_c.at[0])
        result = got_c[0]
        for other in range(1, depth):
            result = result + got_c[other]
        out_ref[...] = result

    @pl.when(jnp.logical_not(is_first) & (core == 1))
    def _():
        with jax.named_scope("level_wait"):
            received(got_c.at[others], recv_c.at[0])
        result = last[1, level]
        for r in range(1, depth):
            result = result + got_c[level ^ r]
        out_ref[...] = result

    def all_sent(blocks):
        ref = panel.at[pl.ds(0, blocks * share)]
        remote(ref, ref, send.at[0], recv_d.at[0], partner).wait_send()

    pairs = plane * depth
    onward = plane + 2 * (depth - 1)
    pl.when(core == 0)(lambda: all_sent(2 * pairs + 1))
    guarded((core == 1) & (spot == 0), lambda: all_sent(2 * pairs - plane - depth + 1 + onward))
    guarded((core == 1) & (spot != 0), lambda: all_sent(2 * pairs - plane - depth + 1 + onward + 1))


def body(panel, row_signs, sample_rows):
    count, width = panel.shape
    hi_count, lo_count = lax.axis_size("hi"), lax.axis_size("lo")
    kept = sample_rows.shape[0]
    share = kept // (hi_count * lo_count)
    side = 2 ** ((lo_count.bit_length() - 1) // 2)
    depth = lo_count // side
    plane = (hi_count // 2) * side
    loads = len(CUTS) - 1
    vmem = pl.BlockSpec(memory_space=pltpu.VMEM)
    dma = pltpu.SemaphoreType.DMA
    f32 = jnp.float32
    chunk = (depth, plane * share, width)
    return pl.pallas_call(
        functools.partial(kernel, hi_count, lo_count),
        out_shape=pltpu.VMEM((share, width), f32),
        in_specs=[pl.BlockSpec(memory_space=pltpu.HBM)] * 4,
        out_specs=vmem,
        scratch_shapes=[
            pltpu.VMEM((count, width), f32),
            pltpu.VMEM((count // LANES, LANES), f32),
            pltpu.SMEM((kept,), jnp.int32),
            pltpu.VMEM((kept // LANES, LANES), jnp.int32),
            pltpu.VMEM((count, width), f32),
            pltpu.VMEM((LANES, 2 * LANES), jnp.bfloat16),
            pltpu.VMEM((count, width), f32),
            pltpu.VMEM((kept, width), f32),
            pltpu.VMEM(chunk, f32),
            pltpu.VMEM(chunk, f32),
            pltpu.VMEM(chunk, f32),
            pltpu.VMEM((2,) + chunk, f32),
            pltpu.VMEM((depth, share, width), f32),
            pltpu.VMEM((2, depth, share, width), f32),
            pltpu.VMEM((2, share, width), f32),
            pltpu.VMEM((2, 2 * plane, share, width), f32),
            pltpu.VMEM((2, share, width), f32),
            pltpu.VMEM((depth, share, width), f32),
            pltpu.VMEM((1, share, width), f32),
            dma((loads,)), dma((3,)),
            dma((1,)), dma((depth,)), dma((2, depth)), dma((1,)),
            dma((2,)), dma((1,)), dma((1,)), pltpu.SemaphoreType.REGULAR((1,)),
        ],
        compiler_params=pltpu.CompilerParams(
            collective_id=0, has_side_effects=True, vmem_limit_bytes=60 * 2**20),
        cost_estimate=pl.CostEstimate(
            flops=2 * count * LOW * 2 * width, bytes_accessed=count * width * 4, transcendentals=0),
    )(panel, row_signs.reshape(count // LANES, LANES), sample_rows,
      sample_rows.reshape(kept // LANES, LANES))


def solution(mesh):
    placed = (P(("hi", "lo"), None), P(("hi", "lo"), None), P())
    return jax.shard_map(
        body, mesh=mesh, in_specs=placed, out_specs=P(("hi", "lo"), None), check_vma=False
    )
```
